512 devices in a mesh: head: 64 (over x_lo, z, core), row: 8 (over y, x_hi).
Axes of the slice: x: 4 (x_hi: 2, x_lo: 2; x = x_hi * 2 + x_lo), y: 4, z: 16, core: 2. Of those that a mesh axis runs over, the one named last changes fastest.
Arguments:
- tokens: bfloat16 [2, 128, 4096], P(None, None, 'row'), may hold values from -6 to 6
- w_zx: bfloat16 [4096, 2, 8192], P('row', None, 'head'), may hold values from -0.09375 to 0.09375
- w_bc: bfloat16 [4096, 2048], P('row', 'head'), may hold values from -0.09375 to 0.09375
- w_dt: bfloat16 [4096, 128], P('row', 'head'), may hold values from -0.09375 to 0.09375
- conv_wx: float32 [4, 8192], P(None, 'head'), may hold values from -3 to 3
- conv_bx: float32 [8192], P('head'), may hold values from -3 to 3
- conv_wbc: float32 [4, 2048], P(None, 'head'), may hold values from -3 to 3
- conv_bbc: float32 [2048], P('head'), may hold values from -3 to 3
- dt_bias: float32 [128], P('head'), may hold values from -2 to 1
- decay_rate: float32 [128], P('head'), may hold values from 0.05 to 4
- skip_gain: float32 [128], P('head'), may hold values from 0.5 to 1.5
- norm_gain: float32 [8192], P('head'), may hold values from 0.5 to 1.5
- w_out: bfloat16 [8192, 4096], P('head', 'row'), may hold values from -0.0625 to 0.0625
- ssm_state: float32 [128, 128, 64, 128], P('row', 'head'), may hold values from -2 to 2
- tail_x: bfloat16 [128, 3, 8192], P('row', None, 'head'), may hold values from -6 to 6
- tail_bc: bfloat16 [128, 3, 2048], P('row', None, 'head'), may hold values from -6 to 6
Outputs:
- layer_out: bfloat16 [2, 128, 4096], P(None, 'head', 'row')
- state_out: float32 [128, 128, 64, 128], P('row', 'head')
- tail_x_out: bfloat16 [128, 3, 8192], P('row', None, 'head')
- tail_bc_out: bfloat16 [128, 3, 2048], P('row', None, 'head')
The draws below stay inside these ranges and needn't reach their ends.
All inputs are finite; a program needn't handle non-finite values.
Results may differ from the reference program's by a relative error of at most 0.015.
Values may be sent and summed in bfloat16 or wider, within the bound.
A program may use at most 64 MiB of HBM per device.

```python
import math
import jax
import jax.numpy as jnp
from jax import lax

D = 4096
H = 128
P_SIZE = 64
N = 128
G = 8
K = 4
STEPS = 2
ROWS = 128


def shard_levels(own_key, extent, split, low, top_value):
    def one(dim, blocks):
        heights = jax.random.uniform(jax.random.fold_in(jax.random.fold_in(own_key, 6), dim), (blocks,), jnp.float32, low / len(split), top_value / len(split))
        return jnp.repeat(jnp.exp(heights), extent[dim] // blocks).reshape((-1,) + (1,) * (len(extent) - dim - 1))

    loudness = one(*split[0])
    for cut in split[1:]:
        loudness = loudness * one(*cut)
    return loudness


def scatter_about(own_key, extent, scale, most, cuts=(), dtype=jnp.bfloat16):
    drawn = jax.random.normal(own_key, extent, jnp.float32) * scale
    if len(cuts) > 0:
        drawn = shard_levels(own_key, extent, cuts, -0.22, 0.18) * drawn
    return jnp.clip(drawn, min=-most, max=most).astype(dtype)


def setup_inputs(seed: int = 0) -> dict:
    key_list = jax.random.split(jax.random.key(seed), 17)
    tokens = scatter_about(key_list[0], (STEPS, ROWS, D), 1.0, 6.0, ((2, 8),))
    w_zx = scatter_about(key_list[1], (D, 2, H * P_SIZE), D ** -0.5, 0.09375, ((0, 8), (2, 64)))
    w_bc = scatter_about(key_list[2], (D, 2 * G * N), D ** -0.5, 0.09375, ((0, 8), (1, 64)))
    w_dt = scatter_about(key_list[3], (D, H), D ** -0.5, 0.09375, ((0, 8), (1, 64)))
    conv_wx = scatter_about(key_list[4], (K, H * P_SIZE), 0.5, 3.0, ((1, 64),), jnp.float32)
    conv_bx = scatter_about(key_list[5], (H * P_SIZE,), 0.5, 3.0, ((0, 64),), jnp.float32)
    conv_wbc = scatter_about(key_list[6], (K, 2 * G * N), 0.5, 3.0, ((1, 64),), jnp.float32)
    conv_bbc = scatter_about(key_list[7], (2 * G * N,), 0.5, 3.0, ((0, 64),), jnp.float32)
    dt_bias = jnp.clip(-2.0 + 3.0 * jax.random.uniform(key_list[8], (H,), jnp.float32) ** shard_levels(key_list[8], (H,), ((0, 64),), -0.2, 0.2), -2.0, 1.0)
    decay_rate = jnp.clip(jnp.exp(math.log(4.0) - 4.3820266 * jax.random.uniform(key_list[9], (H,), jnp.float32) ** shard_levels(key_list[9], (H,), ((0, 64),), -0.2, 0.2)), 0.05, 4.0)
    skip_gain = jnp.clip(0.5 + 1.0 * jax.random.uniform(key_list[10], (H,), jnp.float32) ** shard_levels(key_list[10], (H,), ((0, 64),), -0.2, 0.2), 0.5, 1.5)
    norm_gain = jnp.clip(1.0 + 0.1 * jax.random.normal(key_list[11], (H * P_SIZE,), jnp.float32), 0.5, 1.5)
    w_out = scatter_about(key_list[12], (H * P_SIZE, D), (H * P_SIZE) ** -0.5, 0.0625, ((0, 64), (1, 8)))
    ssm_state = scatter_about(key_list[13], (ROWS, H, P_SIZE, N), 0.3, 2.0, ((0, 8), (1, 64)), jnp.float32)
    tail_x = scatter_about(key_list[14], (ROWS, K - 1, H * P_SIZE), 1.0, 6.0, ((0, 8), (2, 64)))
    tail_bc = scatter_about(key_list[15], (ROWS, K - 1, 2 * G * N), 1.0, 6.0, ((0, 8), (2, 64)))
    return {"tokens": tokens, "w_zx": w_zx, "w_bc": w_bc, "w_dt": w_dt, "conv_wx": conv_wx, "conv_bx": conv_bx, "conv_wbc": conv_wbc, "conv_bbc": conv_bbc, "dt_bias": dt_bias, "decay_rate": decay_rate, "skip_gain": skip_gain, "norm_gain": norm_gain, "w_out": w_out, "ssm_state": ssm_state, "tail_x": tail_x, "tail_bc": tail_bc}


epsilon = 1e-05

def convolve(window, weight, offset):
    summed = lax.optimization_barrier(jnp.sum(window.astype(jnp.float32) * weight[None, :, :], axis=1)) + offset[None, :]
    return jax.nn.silu(summed).astype(jnp.bfloat16)

def reference(tokens, w_zx, w_bc, w_dt, conv_wx, conv_bx, conv_wbc, conv_bbc, dt_bias, decay_rate, skip_gain, norm_gain, w_out, ssm_state, tail_x, tail_bc):
    ssm_now = ssm_state
    neg_rate = -decay_rate
    inner_width = H * P_SIZE
    per_group = H // G
    proj_zx = w_zx.reshape(D, 2 * inner_width)
    results = []
    for which_step in range(STEPS):
        inputs = tokens[which_step]
        row_count = inputs.shape[0]
        gate_up = jnp.dot(inputs, proj_zx, preferred_element_type=jnp.float32).astype(jnp.bfloat16)
        gate_raw = gate_up[:, :inner_width]
        x_raw = gate_up[:, inner_width:]
        bc_raw = jnp.dot(inputs, w_bc, preferred_element_type=jnp.float32).astype(jnp.bfloat16)
        dt_raw = jnp.dot(inputs, w_dt, preferred_element_type=jnp.float32).astype(jnp.bfloat16)
        window_x = jnp.concatenate([tail_x, x_raw[:, None, :]], axis=1)
        conv_x = convolve(window_x, conv_wx, conv_bx)
        tail_x = window_x[:, 1:, :]
        window_bc = jnp.concatenate([tail_bc, bc_raw[:, None, :]], axis=1)
        conv_bc = convolve(window_bc, conv_wbc, conv_bbc)
        tail_bc = window_bc[:, 1:, :]
        b_all = conv_bc[:, :G * N].astype(jnp.float32).reshape(row_count, G, N)
        c_all = conv_bc[:, G * N:].astype(jnp.float32).reshape(row_count, G, N)
        step_size = jax.nn.softplus(dt_raw.astype(jnp.float32) + dt_bias[None, :])
        decay_factor = jnp.exp(step_size * neg_rate[None, :])
        x_heads = conv_x.astype(jnp.float32).reshape(row_count, H, P_SIZE)
        pieces = []
        outputs = []
        for group_index in range(G):
            first_head = group_index * per_group
            last_head = first_head + per_group
            new_piece = decay_factor[:, first_head:last_head, None, None] * ssm_now[:, first_head:last_head]
            new_piece = new_piece + (step_size[:, first_head:last_head, None] * x_heads[:, first_head:last_head])[:, :, :, None] * b_all[:, group_index, None, None, :]
            pieces.append(new_piece)
            outputs.append(jnp.einsum('rhpn,rn->rhp', new_piece, c_all[:, group_index], precision=lax.Precision.HIGHEST))
        ssm_now = jnp.concatenate(pieces, axis=1)
        y_heads = jnp.concatenate(outputs, axis=1) + skip_gain[None, :, None] * x_heads
        gated = y_heads.reshape(row_count, inner_width) * jax.nn.silu(gate_raw.astype(jnp.float32))
        grouped = gated.reshape(row_count, G, inner_width // G)
        mean_sq = lax.optimization_barrier(jnp.sum(grouped * grouped, axis=2)) / (inner_width // G)
        normed = (grouped * lax.rsqrt(mean_sq + epsilon)[:, :, None]).reshape(row_count, inner_width) * norm_gain[None, :]
        normed = normed.astype(jnp.bfloat16)
        results.append(jnp.dot(normed, w_out, preferred_element_type=jnp.float32).astype(jnp.bfloat16))
    return (jnp.stack(results), ssm_now, tail_x, tail_bc)
```

```python
import jax
import jax.numpy as jnp
from jax import lax
from jax.experimental import pallas as pl
from jax.experimental.pallas import tpu as pltpu
from jax.sharding import PartitionSpec as P

MESH = pl.DeviceIdType.MESH
F32 = jnp.float32
BF16 = jnp.bfloat16
EPS = 1e-05
NT = (((1,), (1,)), ((), ()))


def dot(a, b):
    return jnp.dot(a, b, preferred_element_type=F32)


def iota(shape, dim):
    return lax.broadcasted_iota(jnp.int32, shape, dim)


def kernel(
    tokens, w_zx, w_bc, w_dt, w_out, state,
    conv_wx, conv_bx, conv_wbc, conv_bbc, dt_bias, decay_rate, skip_gain, norm_gain, tail_x, tail_bc,
    layer_out, state_out, tail_x_out, tail_bc_out,
    tok, wz, wbc, wdt, st, zf, wa, wgx,
    sa, ra, sb, rb, sc, rc, s3, r3, r4, s5, r5, wo,
    tx, tb, gs, n4, f4, lhs, f5, o5, so,
    lsem, ssem, rsem, wsend, wrecv, csend, crecv, osem,
):
    row = lax.axis_index("row")
    head = lax.axis_index("head")
    grp = lax.div(head, 8)
    mem = lax.rem(head, 8)
    quart = lax.rem(head, 4)
    core = lax.rem(head, 2)
    owner_kind = lax.div(head, 32)
    bc_group = lax.div(lax.rem(head, 32), 4)

    loads = [
        pltpu.make_async_copy(src, dst, lsem.at[n])
        for n, (src, dst) in enumerate(
            ((tokens, tok), (w_bc, wbc), (w_dt, wdt), (w_zx, wz), (state, st))
        )
    ]
    for load in loads:
        load.start()

    barrier = pltpu.get_barrier_semaphore()

    def tell(h, r):
        pl.semaphore_signal(barrier, inc=1, device_id=(h, r), device_id_type=MESH)

    for d in range(1, 8):
        tell(head, lax.rem(row + d, 8))
    for d in range(1, 8):
        tell(grp * 8 + lax.rem(mem + d, 8), row)
    for d in range(1, 8):
        tell(lax.rem(head + 8 * d, 64), row)
    own_source = ((owner_kind == 0) & (grp == bc_group)) | ((owner_kind == 1) & (grp == bc_group))
    for n in range(8):
        src = (n // 4) * 32 + grp * 4 + n % 4

        @pl.when(src != head)
        def _():
            tell(src, row)

    lane = iota((16, 128), 1)
    loads[1].wait()
    spread = (iota((32, 128), 1) % 32 == iota((32, 128), 0)).astype(BF16)
    wa[:, :128] = dot(wbc[...], spread).astype(BF16)
    loads[2].wait()
    wd = wdt[...].astype(F32)
    wa[:, 128:] = jnp.where(iota((512, 128), 1) < 64, wd[:, 0:1], wd[:, 1:2]).astype(BF16)
    loads[0].wait()
    toks = tok[...].reshape(256, 512)
    pa = dot(toks, wa[...])
    for i in range(8):
        for s in range(2):
            sa[i, s * 16 : s * 16 + 16, :] = pa[s * 128 + i * 16 : s * 128 + i * 16 + 16, :128].astype(BF16)
            sb[i, 2, s * 16 : s * 16 + 16, :] = pa[s * 128 + i * 16 : s * 128 + i * 16 + 16, 128:].astype(BF16)

    pl.semaphore_wait(barrier, jnp.where(own_source, 28, 29))

    sends = []

    def send(src, dst, ss, rs, device):
        copy = pltpu.make_async_remote_copy(
            src_ref=src, dst_ref=dst, send_sem=ss, recv_sem=rs, device_id=device, device_id_type=MESH
        )
        copy.start()
        return copy

    for d in range(1, 8):
        to = lax.rem(row + d, 8)
        sends.append(send(sa.at[to], ra.at[row], ssem.at[0, d], rsem.at[0, row], (head, to)))

    loads[3].wait()
    zf[...] = wz[...].astype(F32)
    wgx[:, :128] = zf[pl.ds(0, 512, stride=2), :].astype(BF16)
    wgx[:, 128:] = zf[pl.ds(1, 512, stride=2), :].astype(BF16)
    pz = dot(toks, wgx[...])
    for i in range(8):
        for s in range(2):
            piece = pz[s * 128 + i * 16 : s * 128 + i * 16 + 16, :].astype(BF16)
            sb[i, 0, s * 16 : s * 16 + 16, :] = piece[:, :128]
            sb[i, 1, s * 16 : s * 16 + 16, :] = piece[:, 128:]
    for d in range(1, 8):
        to = lax.rem(row + d, 8)
        sends.append(send(sb.at[to], rb.at[row], ssem.at[1, d], rsem.at[1, row], (head, to)))

    for n in range(8):
        part = w_out.at[:, (n % 2) * 256 : (n % 2) * 256 + 256]
        place = wo.at[n % 2, pl.ds(mem * 128, 128), :]

        @pl.when(mem != n)
        def _():
            send(part, place, wsend.at[n], wrecv.at[mem], (grp * 8 + n, row))

        @pl.when(mem == n)
        def _():
            pltpu.make_async_copy(part, place, wrecv.at[mem]).start()

    ra[row] = sa[row]
    rb[row] = sb[row]

    tx[:, 0:3, :] = tail_x[...].astype(F32)
    narrow = tail_bc[...].astype(F32)
    tb[:, 0:3, :] = jnp.concatenate([narrow] * 4, axis=2)
    txr, tbr = tx.reshape(128, 128), tb.reshape(128, 128)

    def tail(ref, t):
        return ref[pl.ds(t, 16, stride=8), :]

    def windows(ref, raw, weight, bias):
        t0, t1, t2 = tail(ref, 0), tail(ref, 1), tail(ref, 2)
        r0, r1 = raw[:16], raw[16:]
        w = [weight[k : k + 1, :] for k in range(4)]
        c0 = t0 * w[0] + t1 * w[1] + t2 * w[2] + r0 * w[3] + bias
        c1 = t1 * w[0] + t2 * w[1] + r0 * w[2] + r1 * w[3] + bias
        both = jnp.concatenate([c0, c1], axis=0)
        return jax.nn.silu(both).astype(BF16)

    def new_tail(ref, raw):
        ref[pl.ds(0, 16, stride=8), :] = tail(ref, 2)
        ref[pl.ds(1, 16, stride=8), :] = raw[:16]
        ref[pl.ds(2, 16, stride=8), :] = raw[16:]

    weight_bc = jnp.concatenate([conv_wbc[...]] * 4, axis=1)
    bias_bc = jnp.concatenate([conv_bbc[...]] * 4, axis=1)

    def arrived(buf, sem):
        pltpu.make_async_copy(buf, buf, sem).wait()

    for d in range(1, 8):
        frm = lax.rem(row + d, 8)
        arrived(ra.at[frm], rsem.at[0, frm])
    total = ra[0].astype(F32)
    for i in range(1, 8):
        total += ra[i].astype(F32)
    raw_bc = total.astype(BF16).astype(F32)
    conv_bc = windows(tbr, raw_bc, weight_bc, bias_bc).astype(F32)
    sc[...] = jnp.where(lax.div(iota((32, 128), 1), 32) == quart, conv_bc, 0.0).astype(BF16)
    slot = owner_kind * 4 + quart
    for n in range(8):
        to = bc_group * 8 + n

        @pl.when(to != head)
        def _():
            send(sc, rc.at[slot], ssem.at[2, n], rsem.at[2, slot], (to, row))

        @pl.when(to == head)
        def _():
            pltpu.make_async_copy(sc, rc.at[slot], rsem.at[2, slot]).start()

    new_tail(tbr, raw_bc)
    tail_bc_out[...] = tb[:, 0:3, 0:32].astype(BF16)

    for d in range(1, 8):
        frm = lax.rem(row + d, 8)
        arrived(rb.at[frm], rsem.at[1, frm])
    mixed = []
    for part in range(3):
        total = rb[0, part].astype(F32)
        for i in range(1, 8):
            total += rb[i, part].astype(F32)
        mixed.append(total.astype(BF16).astype(F32))
    gate_raw, raw_x, dt_raw = mixed
    xc = windows(txr, raw_x, conv_wx[...], conv_bx[...]).astype(F32)
    new_tail(txr, raw_x)
    tail_x_out[...] = tx[:, 0:3, :].astype(BF16)
    first = iota((1, 128), 1) < 64

    def per_head(ref):
        return jnp.where(first, ref[0], ref[1])

    step_size = jax.nn.softplus(dt_raw + per_head(dt_bias))
    decay = jnp.exp(-step_size * per_head(decay_rate))
    a = step_size * xc
    skip = per_head(skip_gain) * xc
    gate = jax.nn.silu(gate_raw)
    d0, d1 = decay[:16], decay[16:]
    d01 = d0 * d1
    a0, a1 = a[:16], a[16:]
    loads[4].wait()

    for n in range(8):
        arrived(rc.at[n], rsem.at[2, n])
    b = rc[0].astype(F32) + rc[1].astype(F32) + rc[2].astype(F32) + rc[3].astype(F32)
    c = rc[4].astype(F32) + rc[5].astype(F32) + rc[6].astype(F32) + rc[7].astype(F32)
    c_low = c.astype(BF16)
    b0, b1 = b[:16], b[16:]
    c0, c1 = c[:16], c[16:]
    mod16 = iota((32, 128), 0) % 16
    read = jnp.zeros((32, 128), F32)
    for r in range(16):
        one = lax.dot_general(c_low, st[r].astype(BF16), NT, preferred_element_type=F32)
        read = jnp.where(mod16 == r, one, read)

    def along(u, v):
        return jnp.sum(u * v, axis=1, keepdims=True)

    y0 = d0 * read[:16] + a0 * along(b0, c0)
    y1 = d01 * read[16:] + d1 * a0 * along(b0, c1) + a1 * along(b1, c1)
    gated = (jnp.concatenate([y0, y1], axis=0) + skip) * gate
    gs[...] = gated
    s3[...] = jnp.zeros_like(s3)
    s3r = s3.reshape(64, 128)
    for s in range(2):
        for k in range(2):
            s3r[pl.ds(s * 2 + k, 8, stride=8), :] = gs[pl.ds(s * 16 + k, 8, stride=2), :]
    s3r[pl.ds(4, 8, stride=8), :] = jnp.broadcast_to(norm_gain[...], (8, 128))

    for d in range(1, 8):
        to = lax.rem(mem + d, 8)
        sends.append(send(s3.at[to], r3.at[mem], ssem.at[3, d], rsem.at[3, mem], (grp * 8 + to, row)))
    r3[mem] = s3[mem]

    def high_low(v):
        high = v.astype(BF16).astype(F32)
        return [high, (v - high).astype(BF16).astype(F32)]

    d10 = d1 * a0
    zero = jnp.zeros((16, 128), F32)
    columns = jnp.concatenate(
        high_low(d01) + high_low(d10) + high_low(a1) + [zero, zero], axis=0
    )
    columns = jnp.transpose(columns).astype(BF16)
    one = jnp.ones((16, 128), F32)
    left = jnp.concatenate([zero, zero, b0, b0, b1, b1, zero, zero], axis=0)
    right = jnp.concatenate([one, one, zero, zero, zero, zero, zero, zero], axis=0)
    both = jnp.concatenate([left, right], axis=1)
    which = iota((128, 256), 0) % 16

    def update(r):
        picked = jnp.where(which == r, both, 0.0).astype(BF16)
        made = dot(columns, picked)
        so[r] = st[r] * made[:, 128:] + made[:, :128]

    for r in range(8):
        update(r)

    for d in range(1, 8):
        frm = lax.rem(mem + d, 8)
        arrived(r3.at[frm], rsem.at[3, frm])
    square = jnp.zeros((8, 128), F32)
    for n in range(8):
        square += r3[n] * r3[n]
    scale = lax.rsqrt(jnp.sum(square, axis=1, keepdims=True) / 1024.0 + EPS)
    for n in range(8):
        block = r3[n]
        n4[n * 4 : n * 4 + 4, :] = (block * scale * block[4:5, :])[:4]
    r4[row] = n4[...].astype(BF16)
    for d in range(1, 8):
        to = lax.rem(row + d, 8)
        sends.append(send(r4.at[row], r4.at[row], ssem.at[4, d], rsem.at[4, row], (head, to)))

    for n in range(8):
        arrived(wo.at[core, pl.ds(n * 128, 128), :], wrecv.at[n])
    sibling = head + 1 - 2 * core
    sends.append(send(wo.at[core], wo.at[core], csend, crecv, (sibling, row)))

    for r in range(8, 16):
        update(r)
    write = pltpu.make_async_copy(so, state_out, osem)
    write.start()

    for d in range(1, 8):
        frm = lax.rem(row + d, 8)
        arrived(r4.at[frm], rsem.at[4, frm])
    f4[...] = r4[...].reshape(256, 128).astype(F32)
    for n in range(8):
        block = [f4[pl.ds(n * 4 + rr, 8, stride=32), :] for rr in range(4)]
        lhs[:, n * 128 : n * 128 + 128] = jnp.concatenate(block, axis=0).astype(BF16)
    arrived(wo.at[1 - core], crecv)
    f5r = f5.reshape(128, 128)
    for half in range(2):
        out = dot(lhs[...], wo[half])
        for rr in range(4):
            for k in range(2):
                f5r[pl.ds(rr * 4 + half * 2 + k, 8, stride=16), :] = out[rr * 8 : rr * 8 + 8, k * 128 : k * 128 + 128]
    s5[...] = f5[...].astype(BF16)
    for d in range(1, 8):
        to = lax.rem(grp + d, 8)
        sends.append(send(s5.at[to], r5.at[grp], ssem.at[5, d], rsem.at[5, grp], (to * 8 + mem, row)))
    r5[grp] = s5[grp]
    for d in range(1, 8):
        frm = lax.rem(grp + d, 8)
        arrived(r5.at[frm], rsem.at[5, frm])
    total = r5[0].astype(F32)
    for i in range(1, 8):
        total += r5[i].astype(F32)
    o5[...] = total
    for s in range(2):
        for k in range(4):
            pair = o5[pl.ds(s * 8 + k, 2, stride=4), :]
            layer_out[s, :, k * 128 : k * 128 + 128] = pair.astype(BF16)

    for copy in sends:
        copy.wait_send()
    for n in range(8):

        @pl.when(mem != n)
        def _():
            arrived(w_out.at[:, 0:256], wsend.at[n])

        @pl.when(bc_group * 8 + n != head)
        def _():
            arrived(sc, ssem.at[2, n])

    write.wait()


def local(
    tokens, w_zx, w_bc, w_dt, conv_wx, conv_bx, conv_wbc, conv_bbc,
    dt_bias, decay_rate, skip_gain, norm_gain, w_out, ssm_state, tail_x, tail_bc,
):
    hbm = pl.BlockSpec(memory_space=pl.ANY)
    vmem = pl.BlockSpec(memory_space=pltpu.VMEM)
    smem = pl.BlockSpec(memory_space=pltpu.SMEM)
    V = pltpu.VMEM
    dma = pltpu.SemaphoreType.DMA
    outs = pl.pallas_call(
        kernel,
        out_shape=(
            jax.ShapeDtypeStruct((2, 2, 512), BF16),
            jax.ShapeDtypeStruct((16, 128, 128), F32),
            jax.ShapeDtypeStruct((16, 3, 128), BF16),
            jax.ShapeDtypeStruct((16, 3, 32), BF16),
        ),
        in_specs=[hbm] * 6 + [vmem] * 4 + [smem] * 3 + [vmem] * 3,
        out_specs=(vmem, hbm, vmem, vmem),
        scratch_shapes=[
            V((2, 128, 512), BF16),
            V((1024, 128), BF16),
            V((512, 32), BF16),
            V((512, 2), BF16),
            V((16, 128, 128), F32),
            V((1024, 128), F32),
            V((512, 256), BF16),
            V((512, 256), BF16),
            V((8, 32, 128), BF16),
            V((8, 32, 128), BF16),
            V((8, 3, 32, 128), BF16),
            V((8, 3, 32, 128), BF16),
            V((32, 128), BF16),
            V((8, 32, 128), BF16),
            V((8, 8, 128), F32),
            V((8, 8, 128), F32),
            V((8, 32, 128), BF16),
            V((8, 16, 128), BF16),
            V((8, 16, 128), BF16),
            V((2, 1024, 256), BF16),
            V((16, 8, 128), F32),
            V((16, 8, 128), F32),
            V((32, 128), F32),
            V((32, 128), F32),
            V((256, 128), F32),
            V((32, 1024), BF16),
            V((8, 16, 128), F32),
            V((16, 128), F32),
            V((16, 128, 128), F32),
            dma((5,)),
            dma((6, 8)),
            dma((6, 8)),
            dma((8,)),
            dma((8,)),
            dma,
            dma,
            dma,
        ],
        compiler_params=pltpu.CompilerParams(
            collective_id=0, has_side_effects=True, vmem_limit_bytes=40 << 20
        ),
    )(
        tokens,
        w_zx.reshape(1024, 128),
        w_bc,
        w_dt,
        w_out,
        ssm_state.reshape(16, 128, 128),
        conv_wx,
        conv_bx.reshape(1, 128),
        conv_wbc,
        conv_bbc.reshape(1, 32),
        dt_bias,
        decay_rate,
        skip_gain,
        norm_gain.reshape(1, 128),
        tail_x,
        tail_bc,
    )
    return outs[0], outs[1].reshape(16, 2, 64, 128), outs[2], outs[3]


def solution(mesh):
    placed = (
        P(None, None, "row"),
        P("row", None, "head"),
        P("row", "head"),
        P("row", "head"),
        P(None, "head"),
        P("head"),
        P(None, "head"),
        P("head"),
        P("head"),
        P("head"),
        P("head"),
        P("head"),
        P("head", "row"),
        P("row", "head", None, None),
        P("row", None, "head"),
        P("row", None, "head"),
    )
    return jax.shard_map(
        local,
        mesh=mesh,
        in_specs=placed,
        out_specs=(
            P(None, "head", "row"),
            P("row", "head", None, None),
            P("row", None, "head"),
            P("row", None, "head"),
        ),
        check_vma=False,
    )
```

```python
import jax
import jax.numpy as jnp
from jax import lax
from jax.experimental import pallas as pl
from jax.experimental.pallas import tpu as pltpu
from jax.sharding import PartitionSpec as P

MESH = pl.DeviceIdType.MESH
F32 = jnp.float32
BF16 = jnp.bfloat16
EPS = 1e-05
NT = (((1,), (1,)), ((), ()))


def dot(a, b):
    return jnp.dot(a, b, preferred_element_type=F32)


def iota(shape, dim):
    return lax.broadcasted_iota(jnp.int32, shape, dim)


def kernel(
    tokens_h, w_zx_h, w_bc_h, w_dt_h, w_out, state_h,
    conv_wx_h, conv_bx_h, conv_wbc_h, conv_bbc_h, dt_bias_h, decay_rate_h, skip_gain_h, norm_gain_h, tail_x_h, tail_bc_h,
    layer_out, so, tail_x_out, tail_bc_out,
    tok, wz, wbc, wdt, st, conv_wx, conv_bx, conv_wbc, conv_bbc, dt_bias, decay_rate, skip_gain, norm_gain, tail_x, tail_bc,
    zf, wa, wgx,
    sa, ra, sb, rb, sc, rc, s3, r3, r4, s5, r5, wo,
    gs, n4, f4, lhs, f5, o5,
    lsem, ssem, rsem, wsend, wrecv, csend, crecv, near, far,
):
    row = lax.axis_index("row")
    head = lax.axis_index("head")
    grp = lax.div(head, 8)
    mem = lax.rem(head, 8)
    quart = lax.rem(head, 4)
    core = lax.rem(head, 2)
    owner_kind = lax.div(head, 32)
    bc_group = lax.div(lax.rem(head, 32), 4)

    barrier = pltpu.get_barrier_semaphore()

    def signal(sem, h, r):
        pl.semaphore_signal(sem, inc=1, device_id=(h, r), device_id_type=MESH)

    chip = head - core
    for d in range(1, 8):
        signal(barrier, chip, lax.rem(row + d, 8))
    for d in range(1, 4):
        signal(barrier, grp * 8 + lax.rem(mem - core + 2 * d, 8), row)

    @pl.when(core == 1)
    def _():
        signal(barrier, chip, row)

    for d in range(1, 8):
        signal(barrier, lax.rem(chip + 8 * d, 64) + 1, row)
    for n in range(4):
        src = (n // 2) * 32 + grp * 4 + (n % 2) * 2

        @pl.when(src != chip)
        def _():
            signal(barrier, src + 1, row)

    sources = (
        tokens_h, w_bc_h, w_dt_h, w_zx_h, state_h, conv_wbc_h, conv_bbc_h, tail_bc_h,
        conv_wx_h, conv_bx_h, dt_bias_h, decay_rate_h, skip_gain_h, norm_gain_h, tail_x_h,
    )
    targets = (
        tok, wbc, wdt, wz, st, conv_wbc, conv_bbc, tail_bc,
        conv_wx, conv_bx, dt_bias, decay_rate, skip_gain, norm_gain, tail_x,
    )
    loads = [pltpu.make_async_copy(a, b, lsem.at[n]) for n, (a, b) in enumerate(zip(sources, targets))]
    for load in loads:
        load.start()

    loads[1].wait()
    for n in range(4):
        wa[n * 32 : n * 32 + 32, :] = wbc[...]
    loads[2].wait()
    wd = wdt[...].astype(F32)
    wa[128:, :] = jnp.where(iota((128, 512), 0) < 64, wd[0:1], wd[1:2]).astype(BF16)
    loads[0].wait()
    toks = tok[...].reshape(256, 512)
    pa = lax.dot_general(toks, wa[...], NT, preferred_element_type=F32)
    for i in range(8):
        for s in range(2):
            sa[i, s * 16 : s * 16 + 16, :] = pa[s * 128 + i * 16 : s * 128 + i * 16 + 16, :128].astype(BF16)
            sb[i, 2, s * 16 : s * 16 + 16, :] = pa[s * 128 + i * 16 : s * 128 + i * 16 + 16, 128:].astype(BF16)

    @pl.when(core == 0)
    def _():
        pl.semaphore_wait(barrier, 21)
        signal(near, head + 1, row)

    @pl.when(core == 1)
    def _():
        pl.semaphore_wait(near, 1)


    sends = []
    def send(src, dst, ss, rs, device):
        copy = pltpu.make_async_remote_copy(
            src_ref=src, dst_ref=dst, send_sem=ss, recv_sem=rs, device_id=device, device_id_type=MESH
        )
        copy.start()
        return copy

    for d in range(1, 8):
        to = lax.rem(row + d, 8)
        sends.append(send(sa.at[to], ra.at[row], ssem.at[0, d], rsem.at[0, row], (head, to)))

    loads[3].wait()
    zf[...] = wz[...].astype(F32)
    wgx[:, :128] = zf[pl.ds(0, 512, stride=2), :].astype(BF16)
    wgx[:, 128:] = zf[pl.ds(1, 512, stride=2), :].astype(BF16)
    pz = dot(toks, wgx[...])
    for i in range(8):
        for s in range(2):
            piece = pz[s * 128 + i * 16 : s * 128 + i * 16 + 16, :].astype(BF16)
            sb[i, 0, s * 16 : s * 16 + 16, :] = piece[:, :128]
            sb[i, 1, s * 16 : s * 16 + 16, :] = piece[:, 128:]
    for d in range(1, 8):
        to = lax.rem(row + d, 8)
        sends.append(send(sb.at[to], rb.at[row], ssem.at[1, d], rsem.at[1, row], (head, to)))

    for n in range(8):
        part = w_out.at[:, (n % 2) * 256 : (n % 2) * 256 + 256]
        place = wo.at[n % 2, pl.ds(mem * 128, 128), :]

        @pl.when(mem != n)
        def _():
            send(part, place, wsend.at[n], wrecv.at[mem], (grp * 8 + n, row))

        @pl.when(mem == n)
        def _():
            pltpu.make_async_copy(part, place, wrecv.at[mem]).start()

    ra[row] = sa[row]
    rb[row] = sb[row]

    for n in range(5, 15):
        loads[n].wait()

    def windows(t, raw, weight, bias):
        t0, t1, t2 = t
        r0, r1 = raw[:16], raw[16:]
        w = [weight[k : k + 1, :] for k in range(4)]
        c0 = t0 * w[0] + t1 * w[1] + t2 * w[2] + r0 * w[3] + bias
        c1 = t1 * w[0] + t2 * w[1] + r0 * w[2] + r1 * w[3] + bias
        both = jnp.concatenate([c0, c1], axis=0)
        return jax.nn.silu(both).astype(BF16)

    def new_tail(ref, old, raw):
        width = ref.shape[2]
        ref[0] = old[2]
        ref[1] = raw[:16, :width].astype(BF16)
        ref[2] = raw[16:, :width].astype(BF16)

    old_bc = [jnp.concatenate([tail_bc[k].astype(F32)] * 4, axis=1) for k in range(3)]
    old_x = [tail_x[k].astype(F32) for k in range(3)]
    weight_bc = jnp.concatenate([conv_wbc[...]] * 4, axis=1)
    bias_bc = jnp.concatenate([conv_bbc[...]] * 4, axis=1)

    def arrived(buf, sem):
        pltpu.make_async_copy(buf, buf, sem).wait()

    for d in range(1, 8):
        frm = lax.rem(row + d, 8)
        arrived(ra.at[frm], rsem.at[0, frm])
    total = ra[0].astype(F32)
    for i in range(1, 8):
        total += ra[i].astype(F32)
    raw_bc = total.astype(BF16).astype(F32)
    conv_bc = windows(old_bc, raw_bc, weight_bc, bias_bc).astype(F32)
    sc[...] = jnp.where(lax.div(iota((32, 128), 1), 32) == quart, conv_bc, 0.0).astype(BF16)

    @pl.when(core == 1)
    def _():
        pl.semaphore_wait(barrier, jnp.where(grp == bc_group, 20, 22))
        signal(far, head - 1, row)

    @pl.when(core == 0)
    def _():
        pl.semaphore_wait(far, 1)

    slot = owner_kind * 4 + quart
    for n in range(8):
        to = bc_group * 8 + n

        @pl.when(to != head)
        def _():
            send(sc, rc.at[slot], ssem.at[2, n], rsem.at[2, slot], (to, row))

        @pl.when(to == head)
        def _():
            pltpu.make_async_copy(sc, rc.at[slot], rsem.at[2, slot]).start()

    new_tail(tail_bc_out, tail_bc, raw_bc)

    for d in range(1, 8):
        frm = lax.rem(row + d, 8)
        arrived(rb.at[frm], rsem.at[1, frm])
    mixed = []
    for part in range(3):
        total = rb[0, part].astype(F32)
        for i in range(1, 8):
            total += rb[i, part].astype(F32)
        mixed.append(total.astype(BF16).astype(F32))
    gate_raw, raw_x, dt_raw = mixed
    xc = windows(old_x, raw_x, conv_wx[...], conv_bx[...]).astype(F32)
    new_tail(tail_x_out, tail_x, raw_x)
    first = iota((1, 128), 1) < 64

    def per_head(ref):
        return jnp.where(first, ref[:, 0:1], ref[:, 1:2])

    step_size = jax.nn.softplus(dt_raw + per_head(dt_bias))
    decay = jnp.exp(-step_size * per_head(decay_rate))
    a = step_size * xc
    skip = per_head(skip_gain) * xc
    gate = jax.nn.silu(gate_raw)
    d0, d1 = decay[:16], decay[16:]
    d01 = d0 * d1
    a0, a1 = a[:16], a[16:]
    loads[4].wait()

    for n in range(8):
        arrived(rc.at[n], rsem.at[2, n])
    b = rc[0].astype(F32) + rc[1].astype(F32) + rc[2].astype(F32) + rc[3].astype(F32)
    c = rc[4].astype(F32) + rc[5].astype(F32) + rc[6].astype(F32) + rc[7].astype(F32)
    c_low = c.astype(BF16)
    b0, b1 = b[:16], b[16:]
    c0, c1 = c[:16], c[16:]
    mod16 = iota((32, 128), 0) % 16
    read = jnp.zeros((32, 128), F32)
    for r in range(16):
        one = lax.dot_general(c_low, st[r].astype(BF16), NT, preferred_element_type=F32)
        read = jnp.where(mod16 == r, one, read)

    def along(u, v):
        return jnp.sum(u * v, axis=1, keepdims=True)

    y0 = d0 * read[:16] + a0 * along(b0, c0)
    y1 = d01 * read[16:] + d1 * a0 * along(b0, c1) + a1 * along(b1, c1)
    gated = (jnp.concatenate([y0, y1], axis=0) + skip) * gate
    gs[...] = gated
    s3[...] = jnp.zeros_like(s3)
    s3r = s3.reshape(64, 128)
    for s in range(2):
        for k in range(2):
            s3r[pl.ds(s * 2 + k, 8, stride=8), :] = gs[pl.ds(s * 16 + k, 8, stride=2), :]
    s3r[pl.ds(4, 8, stride=8), :] = jnp.broadcast_to(norm_gain[...], (8, 128))

    for d in range(1, 8):
        to = lax.rem(mem + d, 8)
        sends.append(send(s3.at[to], r3.at[mem], ssem.at[3, d], rsem.at[3, mem], (grp * 8 + to, row)))
    r3[mem] = s3[mem]

    def high_low(v):
        high = v.astype(BF16).astype(F32)
        return [high, (v - high).astype(BF16).astype(F32)]

    d10 = d1 * a0
    zero = jnp.zeros((16, 128), F32)
    columns = jnp.concatenate(
        high_low(d01) + high_low(d10) + high_low(a1) + [zero, zero], axis=0
    )
    columns = jnp.transpose(columns).astype(BF16)
    one = jnp.ones((16, 128), F32)
    left = jnp.concatenate([zero, zero, b0, b0, b1, b1, zero, zero], axis=0)
    right = jnp.concatenate([one, one, zero, zero, zero, zero, zero, zero], axis=0)
    both = jnp.concatenate([left, right], axis=1)
    which = iota((128, 256), 0) % 16

    def update(r):
        picked = jnp.where(which == r, both, 0.0).astype(BF16)
        made = dot(columns, picked)
        so[r] = st[r] * made[:, 128:] + made[:, :128]

    for r in range(8):
        update(r)

    for d in range(1, 8):
        frm = lax.rem(mem + d, 8)
        arrived(r3.at[frm], rsem.at[3, frm])
    square = jnp.zeros((8, 128), F32)
    for n in range(8):
        square += r3[n] * r3[n]
    scale = lax.rsqrt(jnp.sum(square, axis=1, keepdims=True) / 1024.0 + EPS)
    for n in range(8):
        block = r3[n]
        n4[n * 4 : n * 4 + 4, :] = (block * scale * block[4:5, :])[:4]
    r4[row] = n4[...].astype(BF16)
    for d in range(1, 8):
        to = lax.rem(row + d, 8)
        sends.append(send(r4.at[row], r4.at[row], ssem.at[4, d], rsem.at[4, row], (head, to)))

    for n in range(8):
        arrived(wo.at[core, pl.ds(n * 128, 128), :], wrecv.at[n])
    sibling = head + 1 - 2 * core
    sends.append(send(wo.at[core], wo.at[core], csend, crecv, (sibling, row)))

    for r in range(8, 16):
        update(r)

    for d in range(1, 8):
        frm = lax.rem(row + d, 8)
        arrived(r4.at[frm], rsem.at[4, frm])
    f4[...] = r4[...].reshape(256, 128).astype(F32)
    for n in range(8):
        block = [f4[pl.ds(n * 4 + rr, 8, stride=32), :] for rr in range(4)]
        lhs[:, n * 128 : n * 128 + 128] = jnp.concatenate(block, axis=0).astype(BF16)
    arrived(wo.at[1 - core], crecv)
    f5r = f5.reshape(128, 128)
    for half in range(2):
        out = dot(lhs[...], wo[half])
        for rr in range(4):
            for k in range(2):
                f5r[pl.ds(rr * 4 + half * 2 + k, 8, stride=16), :] = out[rr * 8 : rr * 8 + 8, k * 128 : k * 128 + 128]
    s5[...] = f5[...].astype(BF16)
    for d in range(1, 8):
        to = lax.rem(grp + d, 8)
        sends.append(send(s5.at[to], r5.at[grp], ssem.at[5, d], rsem.at[5, grp], (to * 8 + mem, row)))
    r5[grp] = s5[grp]
    for d in range(1, 8):
        frm = lax.rem(grp + d, 8)
        arrived(r5.at[frm], rsem.at[5, frm])
    total = r5[0].astype(F32)
    for i in range(1, 8):
        total += r5[i].astype(F32)
    o5[...] = total
    for s in range(2):
        for k in range(4):
            pair = o5[pl.ds(s * 8 + k, 2, stride=4), :]
            layer_out[s, :, k * 128 : k * 128 + 128] = pair.astype(BF16)

    for copy in sends:
        copy.wait_send()
    for n in range(8):

        @pl.when(mem != n)
        def _():
            arrived(w_out.at[:, 0:256], wsend.at[n])

        @pl.when(bc_group * 8 + n != head)
        def _():
            arrived(sc, ssem.at[2, n])


def hand_over(a, b, c, d, oa, ob, oc, od, sem):
    copies = [
        pltpu.make_async_copy(src, dst, sem.at[n])
        for n, (src, dst) in enumerate(((a, oa), (b, ob), (c, oc), (d, od)))
    ]
    for copy in copies:
        copy.start()
    for copy in copies:
        copy.wait()


def local(
    tokens, w_zx, w_bc, w_dt, conv_wx, conv_bx, conv_wbc, conv_bbc,
    dt_bias, decay_rate, skip_gain, norm_gain, w_out, ssm_state, tail_x, tail_bc,
):
    hbm = pl.BlockSpec(memory_space=pltpu.HBM)
    vmem = pl.BlockSpec(memory_space=pltpu.VMEM)
    V = pltpu.VMEM
    dma = pltpu.SemaphoreType.DMA
    shapes = (
        jax.ShapeDtypeStruct((2, 2, 512), BF16),
        jax.ShapeDtypeStruct((16, 128, 128), F32),
        jax.ShapeDtypeStruct((3, 16, 128), BF16),
        jax.ShapeDtypeStruct((3, 16, 32), BF16),
    )
    operands = (
        tokens,
        w_zx.reshape(1024, 128),
        w_bc.T,
        w_dt.T,
        w_out,
        ssm_state.reshape(16, 128, 128),
        conv_wx,
        conv_bx.reshape(1, 128),
        conv_wbc,
        conv_bbc.reshape(1, 32),
        dt_bias.reshape(1, 2),
        decay_rate.reshape(1, 2),
        skip_gain.reshape(1, 2),
        norm_gain.reshape(1, 128),
        jnp.transpose(tail_x, (1, 0, 2)),
        jnp.transpose(tail_bc, (1, 0, 2)),
    )
    made = pl.pallas_call(
        kernel,
        out_shape=tuple(V(v.shape, v.dtype) for v in shapes),
        in_specs=[hbm] * 16,
        out_specs=(vmem,) * 4,
        scratch_shapes=[
            V((2, 128, 512), BF16),
            V((1024, 128), BF16),
            V((32, 512), BF16),
            V((2, 512), BF16),
            V((16, 128, 128), F32),
            V((4, 128), F32),
            V((1, 128), F32),
            V((4, 32), F32),
            V((1, 32), F32),
            V((1, 2), F32),
            V((1, 2), F32),
            V((1, 2), F32),
            V((1, 128), F32),
            V((3, 16, 128), BF16),
            V((3, 16, 32), BF16),
            V((1024, 128), F32),
            V((256, 512), BF16),
            V((512, 256), BF16),
            V((8, 32, 128), BF16),
            V((8, 32, 128), BF16),
            V((8, 3, 32, 128), BF16),
            V((8, 3, 32, 128), BF16),
            V((32, 128), BF16),
            V((8, 32, 128), BF16),
            V((8, 8, 128), F32),
            V((8, 8, 128), F32),
            V((8, 32, 128), BF16),
            V((8, 16, 128), BF16),
            V((8, 16, 128), BF16),
            V((2, 1024, 256), BF16),
            V((32, 128), F32),
            V((32, 128), F32),
            V((256, 128), F32),
            V((32, 1024), BF16),
            V((8, 16, 128), F32),
            V((16, 128), F32),
            dma((15,)),
            dma((6, 8)),
            dma((6, 8)),
            dma((8,)),
            dma((8,)),
            dma,
            dma,
            pltpu.SemaphoreType.REGULAR,
            pltpu.SemaphoreType.REGULAR,
        ],
        compiler_params=pltpu.CompilerParams(
            collective_id=0, has_side_effects=True, vmem_limit_bytes=32 << 20
        ),
    )(*(pltpu.with_memory_space_constraint(v, pltpu.HBM) for v in operands))
    outs = pl.pallas_call(
        hand_over,
        out_shape=shapes,
        in_specs=[pl.BlockSpec(memory_space=pl.ANY)] * 4,
        out_specs=(hbm,) * 4,
        scratch_shapes=[dma((4,))],
        compiler_params=pltpu.CompilerParams(vmem_limit_bytes=32 << 20),
    )(*made)
    back = (1, 0, 2)
    return outs[0], outs[1].reshape(16, 2, 64, 128), jnp.transpose(outs[2], back), jnp.transpose(outs[3], back)


def solution(mesh):
    placed = (
        P(None, None, "row"),
        P("row", None, "head"),
        P("row", "head"),
        P("row", "head"),
        P(None, "head"),
        P("head"),
        P(None, "head"),
        P("head"),
        P("head"),
        P("head"),
        P("head"),
        P("head"),
        P("head", "row"),
        P("row", "head", None, None),
        P("row", None, "head"),
        P("row", None, "head"),
    )
    return jax.shard_map(
        local,
        mesh=mesh,
        in_specs=placed,
        out_specs=(
            P(None, "head", "row"),
            P("row", "head", None, None),
            P("row", None, "head"),
            P("row", None, "head"),
        ),
        check_vma=False,
    )
```

```python
import jax
import jax.numpy as jnp
from jax import lax
from jax.experimental import pallas as pl
from jax.experimental.pallas import tpu as pltpu
from jax.sharding import PartitionSpec as P

MESH = pl.DeviceIdType.MESH
F32 = jnp.float32
BF16 = jnp.bfloat16
EPS = 1e-05
NT = (((1,), (1,)), ((), ()))


def dot(a, b):
    return jnp.dot(a, b, preferred_element_type=F32)


def iota(shape, dim):
    return lax.broadcasted_iota(jnp.int32, shape, dim)


def kernel(
    tokens_h, w_zx_h, w_bc_h, w_dt_h, w_out, state_h,
    conv_wx_h, conv_bx_h, conv_wbc_h, conv_bbc_h, dt_bias_h, decay_rate_h, skip_gain_h, norm_gain_h, tail_x_h, tail_bc_h,
    layer_out, so, tail_x_out, tail_bc_out,
    tok, wz, wbc, wdt, st, conv_wx, conv_bx, conv_wbc, conv_bbc, dt_bias, decay_rate, skip_gain, norm_gain, tail_x, tail_bc,
    zf, wa, wgx,
    sa, ra, sb, rb, sc, rc, s3, r3, r4, s5, r5, wo,
    gs, f4, lhs, f5, o5,
    lsem, ssem, rsem, wsend, wrecv, csend, crecv, near, far, xsend, xrecv,
):
    row = lax.axis_index("row")
    head = lax.axis_index("head")
    grp = lax.div(head, 8)
    mem = lax.rem(head, 8)
    quad = lax.div(head, 4)
    place = lax.rem(head, 4)
    core = lax.rem(head, 2)
    owner_kind = lax.div(head, 32)
    bc_group = lax.div(lax.rem(head, 32), 4)

    barrier = pltpu.get_barrier_semaphore()

    def signal(sem, h, r):
        pl.semaphore_signal(sem, inc=1, device_id=(h, r), device_id_type=MESH)

    chip = head - core
    for d in range(1, 8):
        signal(barrier, chip, lax.rem(row + d, 8))
    other = quad * 4 + lax.rem(place - core + 2, 4)
    signal(barrier, other, row)

    @pl.when(core == 1)
    def _():
        signal(barrier, chip, row)

    for d in range(1, 16):
        signal(barrier, lax.rem(chip + 4 * d, 64) + 1, row)
    signal(barrier, grp * 8 + lax.rem(mem - core + 4 + 2 - 4 * lax.div(lax.rem(mem, 4), 2), 8) + 1, row)
    for n in range(4):
        src = (n // 2) * 32 + grp * 4 + (n % 2) * 2

        @pl.when(src != chip)
        def _():
            signal(barrier, src + 1, row)

    sources = (
        tokens_h, w_bc_h, w_dt_h, w_zx_h, state_h, conv_wbc_h, conv_bbc_h, tail_bc_h,
        conv_wx_h, conv_bx_h, dt_bias_h, decay_rate_h, skip_gain_h, norm_gain_h, tail_x_h,
    )
    targets = (
        tok, wbc, wdt, wz, st, conv_wbc, conv_bbc, tail_bc,
        conv_wx, conv_bx, dt_bias, decay_rate, skip_gain, norm_gain, tail_x,
    )
    loads = [pltpu.make_async_copy(a, b, lsem.at[n]) for n, (a, b) in enumerate(zip(sources, targets))]
    for load in loads:
        load.start()

    loads[1].wait()
    loads[2].wait()
    steps = jnp.concatenate([wdt[...].astype(F32), jnp.zeros((30, 512), F32)], axis=0).astype(BF16)
    for n in range(2):
        wa[n * 64 : n * 64 + 32, :] = wbc[...]
        wa[n * 64 + 32 : n * 64 + 64, :] = steps
    loads[0].wait()
    toks = tok[...].reshape(256, 512)
    pa = lax.dot_general(toks, wa[...], NT, preferred_element_type=F32)
    pa = jnp.where(iota((128, 128), 1) < 64, pa[:128], pa[128:]).astype(BF16)
    for i in range(8):
        sa[i] = pa[i * 16 : i * 16 + 16]

    @pl.when(core == 0)
    def _():
        pl.semaphore_wait(barrier, 17)
        signal(near, head + 1, row)

    @pl.when(core == 1)
    def _():
        pl.semaphore_wait(near, 1)


    sends = []
    def send(src, dst, ss, rs, device):
        copy = pltpu.make_async_remote_copy(
            src_ref=src, dst_ref=dst, send_sem=ss, recv_sem=rs, device_id=device, device_id_type=MESH
        )
        copy.start()
        return copy

    for d in range(1, 8):
        to = lax.rem(row + d, 8)
        sends.append(send(sa.at[to], ra.at[row], ssem.at[0, d], rsem.at[0, row], (head, to)))

    loads[3].wait()
    zf[...] = wz[...].astype(F32)
    wgx[:, :128] = zf[pl.ds(0, 512, stride=2), :].astype(BF16)
    wgx[:, 128:] = zf[pl.ds(1, 512, stride=2), :].astype(BF16)
    pz = dot(toks, wgx[...])
    for i in range(8):
        for s in range(2):
            piece = pz[s * 128 + i * 16 : s * 128 + i * 16 + 16, :].astype(BF16)
            sb[i, 0, s * 16 : s * 16 + 16, :] = piece[:, :128]
            sb[i, 1, s * 16 : s * 16 + 16, :] = piece[:, 128:]
    for d in range(1, 8):
        to = lax.rem(row + d, 8)
        sends.append(send(sb.at[to], rb.at[row], ssem.at[1, d], rsem.at[1, row], (head, to)))

    for n in range(4):
        part = w_out.at[:, (n % 2) * 256 : (n % 2) * 256 + 256]
        spot = wo.at[n % 2, pl.ds(place * 128, 128), :]

        @pl.when(place != n)
        def _():
            send(part, spot, wsend.at[n], wrecv.at[place], (quad * 4 + n, row))

        @pl.when(place == n)
        def _():
            pltpu.make_async_copy(part, spot, wrecv.at[place]).start()

    ra[row] = sa[row]
    rb[row] = sb[row]

    for n in range(5, 15):
        loads[n].wait()

    def taps(window, weight, bias):
        summed = bias
        for k in range(4):
            summed = summed + window[k] * weight[k : k + 1, :]
        return jax.nn.silu(summed).astype(BF16).astype(F32)

    old_bc = [jnp.concatenate([tail_bc[k].astype(F32)] * 4, axis=1) for k in range(3)]
    old_x = [tail_x[k].astype(F32) for k in range(3)]
    weight_bc = jnp.concatenate([conv_wbc[...]] * 4, axis=1)
    bias_bc = jnp.concatenate([conv_bbc[...]] * 4, axis=1)

    def arrived(buf, sem):
        pltpu.make_async_copy(buf, buf, sem).wait()

    for d in range(1, 8):
        frm = lax.rem(row + d, 8)
        arrived(ra.at[frm], rsem.at[0, frm])
    total = ra[0].astype(F32)
    for i in range(1, 8):
        total += ra[i].astype(F32)
    raw = total.astype(BF16).astype(F32)
    lane = iota((16, 128), 1)
    low = lane < 64
    raw_bc = jnp.where(lane % 64 < 32, raw, pltpu.roll(raw, 32, 1))
    window = (
        jnp.where(low, old_bc[0], old_bc[1]),
        jnp.where(low, old_bc[1], old_bc[2]),
        jnp.where(low, old_bc[2], pltpu.roll(raw_bc, 64, 1)),
        raw_bc,
    )
    conv_bc = taps(window, weight_bc, bias_bc)
    sc[...] = jnp.where(lax.rem(lax.div(lane, 32), 2) == lax.rem(place, 2), conv_bc, 0.0).astype(BF16)

    @pl.when(core == 1)
    def _():
        pl.semaphore_wait(barrier, jnp.where(grp == bc_group, 38, 40))
        signal(far, head - 1, row)

    @pl.when(core == 0)
    def _():
        pl.semaphore_wait(far, 1)

    slot = owner_kind * 4 + place
    for n in range(8):
        to = bc_group * 8 + n

        @pl.when(to != head)
        def _():
            send(sc, rc.at[slot], ssem.at[2, n], rsem.at[2, slot], (to, row))

        @pl.when(to == head)
        def _():
            pltpu.make_async_copy(sc, rc.at[slot], rsem.at[2, slot]).start()

    tail_bc_out[0] = tail_bc[2]
    tail_bc_out[1] = raw[:, :32].astype(BF16)
    tail_bc_out[2] = pltpu.roll(raw, 64, 1)[:, :32].astype(BF16)

    for d in range(1, 8):
        frm = lax.rem(row + d, 8)
        arrived(rb.at[frm], rsem.at[1, frm])
    mixed = []
    for part in range(2):
        total = rb[0, part].astype(F32)
        for i in range(1, 8):
            total += rb[i, part].astype(F32)
        mixed.append(total.astype(BF16).astype(F32))
    gate_raw, raw_x = mixed
    x0, x1 = raw_x[:16], raw_x[16:]
    xc0 = taps((old_x[0], old_x[1], old_x[2], x0), conv_wx[...], conv_bx[...])
    xc1 = taps((old_x[1], old_x[2], x0, x1), conv_wx[...], conv_bx[...])
    xc = jnp.concatenate([xc0, xc1], axis=0)
    tail_x_out[0] = tail_x[2]
    tail_x_out[1] = x0.astype(BF16)
    tail_x_out[2] = x1.astype(BF16)
    first = iota((1, 128), 1) < 64

    def per_head(ref):
        return jnp.where(first, ref[:, 0:1], ref[:, 1:2])

    dt_raw = jnp.concatenate(
        [jnp.where(first, raw[:, k : k + 1], raw[:, k + 1 : k + 2]) for k in (32, 96)], axis=0
    )
    step_size = jax.nn.softplus(dt_raw + per_head(dt_bias))
    decay = jnp.exp(-step_size * per_head(decay_rate))
    a = step_size * xc
    skip = per_head(skip_gain) * xc
    gate = jax.nn.silu(gate_raw)
    d0, d1 = decay[:16], decay[16:]
    d01 = d0 * d1
    a0, a1 = a[:16], a[16:]
    loads[4].wait()

    for n in range(8):
        arrived(rc.at[n], rsem.at[2, n])
    def channels(k):
        u = rc[k].astype(F32) + rc[k + 1].astype(F32)
        v = rc[k + 2].astype(F32) + rc[k + 3].astype(F32)
        return jnp.where(low, u, pltpu.roll(v, 64, 1)), jnp.where(low, pltpu.roll(u, 64, 1), v)

    b0, b1 = channels(0)
    c0, c1 = channels(4)
    c_low = jnp.concatenate([c0, c1], axis=0).astype(BF16)
    mod16 = iota((32, 128), 0) % 16
    read = jnp.zeros((32, 128), F32)
    for r in range(16):
        one = lax.dot_general(c_low, st[r].astype(BF16), NT, preferred_element_type=F32)
        read = jnp.where(mod16 == r, one, read)

    def along(u, v):
        return jnp.sum(u * v, axis=1, keepdims=True)

    y0 = d0 * read[:16] + a0 * along(b0, c0)
    y1 = d01 * read[16:] + d1 * a0 * along(b0, c1) + a1 * along(b1, c1)
    gated = (jnp.concatenate([y0, y1], axis=0) + skip) * gate
    gs[...] = gated
    s3[...] = jnp.zeros_like(s3)
    s3r = s3.reshape(64, 128)
    for k in range(8):
        p, t, u = k // 4, k // 2 % 2, k % 2
        s3r[pl.ds(k, 4, stride=16), :] = gs[pl.ds(t * 16 + p * 8 + u, 4, stride=2), :]
    s3r[pl.ds(8, 4, stride=16), :] = jnp.broadcast_to(norm_gain[...], (4, 128))

    for d in range(1, 8):
        to = lax.rem(mem + d, 8)
        sends.append(send(s3.at[lax.rem(to, 4)], r3.at[mem], ssem.at[3, d], rsem.at[3, mem], (grp * 8 + to, row)))
    r3[mem] = s3[place]

    def high_low(v):
        high = v.astype(BF16).astype(F32)
        return [high, (v - high).astype(BF16).astype(F32)]

    d10 = d1 * a0
    zero = jnp.zeros((16, 128), F32)
    columns = jnp.concatenate(
        high_low(d01) + high_low(d10) + high_low(a1) + [zero, zero], axis=0
    )
    columns = jnp.transpose(columns).astype(BF16)
    one = jnp.ones((16, 128), F32)
    left = jnp.concatenate([zero, zero, b0, b0, b1, b1, zero, zero], axis=0)
    right = jnp.concatenate([one, one, zero, zero, zero, zero, zero, zero], axis=0)
    both = jnp.concatenate([left, right], axis=1)
    which = iota((128, 256), 0) % 16

    def update(r):
        picked = jnp.where(which == r, both, 0.0).astype(BF16)
        made = dot(columns, picked)
        so[r] = st[r] * made[:, 128:] + made[:, :128]

    for r in range(8):
        update(r)

    for d in range(1, 8):
        frm = lax.rem(mem + d, 8)
        arrived(r3.at[frm], rsem.at[3, frm])
    square = jnp.zeros((8, 128), F32)
    for n in range(8):
        square += r3[n, 0:8, :] * r3[n, 0:8, :]
    scale = lax.rsqrt(jnp.sum(square, axis=1, keepdims=True) / 1024.0 + EPS)
    blocks = [r3[lax.div(mem, 4) * 4 + n] for n in range(4)]
    r4[row] = jnp.concatenate([v[0:8] * scale * v[8:9] for v in blocks], axis=0).astype(BF16)
    for d in range(1, 8):
        to = lax.rem(row + d, 8)
        sends.append(send(r4.at[row], r4.at[row], ssem.at[4, d], rsem.at[4, row], (head, to)))

    for n in range(4):
        arrived(wo.at[core, pl.ds(n * 128, 128), :], wrecv.at[n])
    sibling = head + 1 - 2 * core
    sends.append(send(wo.at[core], wo.at[core], csend, crecv, (sibling, row)))

    for r in range(8, 16):
        update(r)

    for d in range(1, 8):
        frm = lax.rem(row + d, 8)
        arrived(r4.at[frm], rsem.at[4, frm])
    f4[...] = r4[...].reshape(256, 128).astype(F32)
    for n in range(4):
        block = [f4[pl.ds(n * 8 + k, 8, stride=32), :] for k in range(8)]
        lhs[:, n * 128 : n * 128 + 128] = jnp.concatenate(block, axis=0).astype(BF16)
    arrived(wo.at[1 - core], crecv)
    f5r = f5.reshape(256, 128)
    for half in range(2):
        out = dot(lhs[...], wo[half])
        for n in range(8):
            for k in range(2):
                at = n // 4 * 16 + n % 4 * 4 + half * 2 + k
                f5r[pl.ds(at, 8, stride=32), :] = out[n * 8 : n * 8 + 8, k * 128 : k * 128 + 128]
    s5[...] = f5[...].astype(BF16)
    for d in range(1, 16):
        to = lax.rem(quad + d, 16)
        sends.append(send(s5.at[to], r5.at[quad], xsend.at[d], xrecv.at[quad], (to * 4 + place, row)))
    r5[quad] = s5[quad]
    for d in range(1, 16):
        frm = lax.rem(quad + d, 16)
        arrived(r5.at[frm], xrecv.at[frm])
    total = r5[0].astype(F32)
    for i in range(1, 16):
        total += r5[i].astype(F32)
    o5[...] = total
    for s in range(2):
        for k in range(4):
            pair = o5[pl.ds(s * 8 + k, 2, stride=4), :]
            layer_out[s, :, k * 128 : k * 128 + 128] = pair.astype(BF16)

    for copy in sends:
        copy.wait_send()
    for n in range(4):

        @pl.when(place != n)
        def _():
            arrived(w_out.at[:, 0:256], wsend.at[n])

    for n in range(8):

        @pl.when(bc_group * 8 + n != head)
        def _():
            arrived(sc, ssem.at[2, n])


def hand_over(a, b, c, d, oa, ob, oc, od, sem):
    copies = [
        pltpu.make_async_copy(src, dst, sem.at[n])
        for n, (src, dst) in enumerate(((a, oa), (b, ob), (c, oc), (d, od)))
    ]
    for copy in copies:
        copy.start()
    for copy in copies:
        copy.wait()


def local(
    tokens, w_zx, w_bc, w_dt, conv_wx, conv_bx, conv_wbc, conv_bbc,
    dt_bias, decay_rate, skip_gain, norm_gain, w_out, ssm_state, tail_x, tail_bc,
):
    hbm = pl.BlockSpec(memory_space=pltpu.HBM)
    vmem = pl.BlockSpec(memory_space=pltpu.VMEM)
    V = pltpu.VMEM
    dma = pltpu.SemaphoreType.DMA
    shapes = (
        jax.ShapeDtypeStruct((2, 2, 512), BF16),
        jax.ShapeDtypeStruct((16, 128, 128), F32),
        jax.ShapeDtypeStruct((3, 16, 128), BF16),
        jax.ShapeDtypeStruct((3, 16, 32), BF16),
    )
    operands = (
        tokens,
        w_zx.reshape(1024, 128),
        w_bc.T,
        w_dt.T,
        w_out,
        ssm_state.reshape(16, 128, 128),
        conv_wx,
        conv_bx.reshape(1, 128),
        conv_wbc,
        conv_bbc.reshape(1, 32),
        dt_bias.reshape(1, 2),
        decay_rate.reshape(1, 2),
        skip_gain.reshape(1, 2),
        norm_gain.reshape(1, 128),
        jnp.transpose(tail_x, (1, 0, 2)),
        jnp.transpose(tail_bc, (1, 0, 2)),
    )
    made = pl.pallas_call(
        kernel,
        out_shape=tuple(V(v.shape, v.dtype) for v in shapes),
        in_specs=[hbm] * 16,
        out_specs=(vmem,) * 4,
        scratch_shapes=[
            V((2, 128, 512), BF16),
            V((1024, 128), BF16),
            V((32, 512), BF16),
            V((2, 512), BF16),
            V((16, 128, 128), F32),
            V((4, 128), F32),
            V((1, 128), F32),
            V((4, 32), F32),
            V((1, 32), F32),
            V((1, 2), F32),
            V((1, 2), F32),
            V((1, 2), F32),
            V((1, 128), F32),
            V((3, 16, 128), BF16),
            V((3, 16, 32), BF16),
            V((1024, 128), F32),
            V((128, 512), BF16),
            V((512, 256), BF16),
            V((8, 16, 128), BF16),
            V((8, 16, 128), BF16),
            V((8, 2, 32, 128), BF16),
            V((8, 2, 32, 128), BF16),
            V((16, 128), BF16),
            V((8, 16, 128), BF16),
            V((4, 16, 128), F32),
            V((8, 16, 128), F32),
            V((8, 32, 128), BF16),
            V((16, 16, 128), BF16),
            V((16, 16, 128), BF16),
            V((2, 512, 256), BF16),
            V((32, 128), F32),
            V((256, 128), F32),
            V((64, 512), BF16),
            V((16, 16, 128), F32),
            V((16, 128), F32),
            dma((15,)),
            dma((5, 8)),
            dma((5, 8)),
            dma((4,)),
            dma((4,)),
            dma,
            dma,
            pltpu.SemaphoreType.REGULAR,
            pltpu.SemaphoreType.REGULAR,
            dma((16,)),
            dma((16,)),
        ],
        compiler_params=pltpu.CompilerParams(
            collective_id=0, has_side_effects=True, vmem_limit_bytes=32 << 20
        ),
    )(*(pltpu.with_memory_space_constraint(v, pltpu.HBM) for v in operands))
    outs = pl.pallas_call(
        hand_over,
        out_shape=shapes,
        in_specs=[pl.BlockSpec(memory_space=pl.ANY)] * 4,
        out_specs=(hbm,) * 4,
        scratch_shapes=[dma((4,))],
        compiler_params=pltpu.CompilerParams(vmem_limit_bytes=32 << 20),
    )(*made)
    back = (1, 0, 2)
    return outs[0], outs[1].reshape(16, 2, 64, 128), jnp.transpose(outs[2], back), jnp.transpose(outs[3], back)


def solution(mesh):
    placed = (
        P(None, None, "row"),
        P("row", None, "head"),
        P("row", "head"),
        P("row", "head"),
        P(None, "head"),
        P("head"),
        P(None, "head"),
        P("head"),
        P("head"),
        P("head"),
        P("head"),
        P("head"),
        P("head", "row"),
        P("row", "head", None, None),
        P("row", None, "head"),
        P("row", None, "head"),
    )
    return jax.shard_map(
        local,
        mesh=mesh,
        in_specs=placed,
        out_specs=(
            P(None, "head", "row"),
            P("row", "head", None, None),
            P("row", None, "head"),
            P("row", None, "head"),
        ),
        check_vma=False,
    )
```

```python
import jax
import jax.numpy as jnp
from jax import lax
from jax.experimental import pallas as pl
from jax.experimental.pallas import tpu as pltpu
from jax.sharding import PartitionSpec as P

MESH = pl.DeviceIdType.MESH
F32 = jnp.float32
BF16 = jnp.bfloat16
EPS = 1e-05
NT = (((1,), (1,)), ((), ()))


def dot(a, b):
    return jnp.dot(a, b, preferred_element_type=F32)


def iota(shape, dim):
    return lax.broadcasted_iota(jnp.int32, shape, dim)


def kernel(
    tokens_h, w_zx_h, w_bc_h, w_dt_h, w_out, state_h,
    conv_wx_h, conv_bx_h, conv_wbc_h, conv_bbc_h, dt_bias_h, decay_rate_h, skip_gain_h, norm_gain_h, tail_x_h, tail_bc_h,
    parts, squares, so, tail_x_out, tail_bc_out,
    tok, wz, wbc, wdt, st, conv_wx, conv_bx, conv_wbc, conv_bbc, dt_bias, decay_rate, skip_gain, norm_gain, tail_x, tail_bc,
    zf, wa, wgx,
    sa, ra, sb, rb, sc, rc, s3, s3b, r3, r4, s5, r5, sq, rq, wo,
    gs, f4, lhs, f5, sl,
    lsem, ssem, rsem, wsend, wrecv, csend, crecv, near, far, xsend, xrecv, qsend, qrecv,
):
    row = lax.axis_index("row")
    head = lax.axis_index("head")
    grp = lax.div(head, 8)
    mem = lax.rem(head, 8)
    quad = lax.div(head, 4)
    place = lax.rem(head, 4)
    core = lax.rem(head, 2)
    owner_kind = lax.div(head, 32)
    bc_group = lax.div(lax.rem(head, 32), 4)

    sources = (
        tokens_h, w_bc_h, w_dt_h, w_zx_h, state_h, conv_wbc_h, conv_bbc_h, tail_bc_h,
        conv_wx_h, conv_bx_h, dt_bias_h, decay_rate_h, skip_gain_h, norm_gain_h, tail_x_h,
    )
    targets = (
        tok, wbc, wdt, wz, st, conv_wbc, conv_bbc, tail_bc,
        conv_wx, conv_bx, dt_bias, decay_rate, skip_gain, norm_gain, tail_x,
    )
    loads = [pltpu.make_async_copy(a, b, lsem.at[n]) for n, (a, b) in enumerate(zip(sources, targets))]
    for load in loads[:3]:
        load.start()

    barrier = pltpu.get_barrier_semaphore()

    def signal(sem, h, r):
        pl.semaphore_signal(sem, inc=1, device_id=(h, r), device_id_type=MESH)

    def row_peer(dy, dx):
        return lax.rem(row - x_hi + 2 * dy, 8) + lax.rem(x_hi + dx, 2)

    x_hi = lax.rem(row, 2)
    row_peers = [row_peer(dy, dx) for dy, dx in ((2, 1), (1, 1), (3, 1), (2, 0), (0, 1), (1, 0), (3, 0))]
    chip = head - core
    for peer in row_peers:
        signal(barrier, chip, peer)
    other = quad * 4 + lax.rem(place - core + 2, 4)
    signal(barrier, other, row)

    @pl.when(core == 1)
    def _():
        signal(barrier, chip, row)

    for load in loads[3:]:
        load.start()
    for d in range(1, 16):
        signal(barrier, lax.rem(chip + 4 * d, 64) + 1, row)
    for n in range(4):
        src = (n // 2) * 32 + grp * 4 + (n % 2) * 2

        @pl.when(src != chip)
        def _():
            signal(barrier, src + 1, row)

    loads[1].wait()
    loads[2].wait()
    steps = jnp.concatenate([wdt[...].astype(F32), jnp.zeros((30, 512), F32)], axis=0).astype(BF16)
    for n in range(2):
        wa[n * 64 : n * 64 + 32, :] = wbc[...]
        wa[n * 64 + 32 : n * 64 + 64, :] = steps
    loads[0].wait()
    toks = tok[...].reshape(256, 512)
    pa = lax.dot_general(toks, wa[...], NT, preferred_element_type=F32)
    pa = jnp.where(iota((128, 128), 1) < 64, pa[:128], pa[128:]).astype(BF16)
    for i in range(8):
        sa[i] = pa[i * 16 : i * 16 + 16]

    @pl.when(core == 0)
    def _():
        pl.semaphore_wait(barrier, 17)
        signal(near, head + 1, row)

    @pl.when(core == 1)
    def _():
        pl.semaphore_wait(near, 1)


    def send(src, dst, ss, rs, device):
        copy = pltpu.make_async_remote_copy(
            src_ref=src, dst_ref=dst, send_sem=ss, recv_sem=rs, device_id=device, device_id_type=MESH
        )
        copy.start()
        return copy

    for to in row_peers:
        send(sa.at[to], ra.at[row], ssem.at[0], rsem.at[0], (head, to))

    loads[3].wait()
    zf[...] = wz[...].astype(F32)
    wgx[:, :128] = zf[pl.ds(0, 512, stride=2), :].astype(BF16)
    wgx[:, 128:] = zf[pl.ds(1, 512, stride=2), :].astype(BF16)
    pz = dot(toks, wgx[...])
    for i in range(8):
        for s in range(2):
            piece = pz[s * 128 + i * 16 : s * 128 + i * 16 + 16, :].astype(BF16)
            sb[i, 0, s * 16 : s * 16 + 16, :] = piece[:, :128]
            sb[i, 1, s * 16 : s * 16 + 16, :] = piece[:, 128:]
    for to in row_peers:
        send(sb.at[to], rb.at[row], ssem.at[1], rsem.at[1], (head, to))

    for n in range(4):
        part = w_out.at[:, (n % 2) * 256 : (n % 2) * 256 + 256]
        spot = wo.at[n % 2, pl.ds(place * 128, 128), :]

        @pl.when(place != n)
        def _():
            send(part, spot, wsend, wrecv, (quad * 4 + n, row))

        @pl.when(place == n)
        def _():
            pltpu.make_async_copy(part, spot, wrecv).start()

    ra[row] = sa[row]
    rb[row] = sb[row]

    for n in range(5, 15):
        loads[n].wait()

    def taps(window, weight, bias):
        summed = bias
        for k in range(4):
            summed = summed + window[k] * weight[k : k + 1, :]
        return jax.nn.silu(summed).astype(BF16).astype(F32)

    old_bc = [jnp.concatenate([tail_bc[k].astype(F32)] * 4, axis=1) for k in range(3)]
    old_x = [tail_x[k].astype(F32) for k in range(3)]
    weight_bc = jnp.concatenate([conv_wbc[...]] * 4, axis=1)
    bias_bc = jnp.concatenate([conv_bbc[...]] * 4, axis=1)

    def arrived(buf, sem):
        pltpu.make_async_copy(buf, buf, sem).wait()

    arrived(ra.at[0:7], rsem.at[0])
    total = ra[0].astype(F32)
    for i in range(1, 8):
        total += ra[i].astype(F32)
    raw = total.astype(BF16).astype(F32)
    lane = iota((16, 128), 1)
    low = lane < 64
    raw_bc = jnp.where(lane % 64 < 32, raw, pltpu.roll(raw, 32, 1))
    window = (
        jnp.where(low, old_bc[0], old_bc[1]),
        jnp.where(low, old_bc[1], old_bc[2]),
        jnp.where(low, old_bc[2], pltpu.roll(raw_bc, 64, 1)),
        raw_bc,
    )
    conv_bc = taps(window, weight_bc, bias_bc)
    sc[...] = jnp.where(lax.rem(lax.div(lane, 32), 2) == lax.rem(place, 2), conv_bc, 0.0).astype(BF16)

    @pl.when(core == 1)
    def _():
        pl.semaphore_wait(barrier, jnp.where(grp == bc_group, 36, 38))
        signal(far, head - 1, row)

    @pl.when(core == 0)
    def _():
        pl.semaphore_wait(far, 1)

    slot = owner_kind * 4 + place
    for n in range(8):
        to = bc_group * 8 + n

        @pl.when(to != head)
        def _():
            send(sc, rc.at[slot], ssem.at[2], rsem.at[2], (to, row))

        @pl.when(to == head)
        def _():
            pltpu.make_async_copy(sc, rc.at[slot], rsem.at[2]).start()

    tail_bc_out[0] = tail_bc[2]
    tail_bc_out[1] = raw[:, :32].astype(BF16)
    tail_bc_out[2] = pltpu.roll(raw, 64, 1)[:, :32].astype(BF16)

    arrived(rb.at[0:7], rsem.at[1])
    mixed = []
    for part in range(2):
        total = rb[0, part].astype(F32)
        for i in range(1, 8):
            total += rb[i, part].astype(F32)
        mixed.append(total.astype(BF16).astype(F32))
    gate_raw, raw_x = mixed
    x0, x1 = raw_x[:16], raw_x[16:]
    xc0 = taps((old_x[0], old_x[1], old_x[2], x0), conv_wx[...], conv_bx[...])
    xc1 = taps((old_x[1], old_x[2], x0, x1), conv_wx[...], conv_bx[...])
    xc = jnp.concatenate([xc0, xc1], axis=0)
    tail_x_out[0] = tail_x[2]
    tail_x_out[1] = x0.astype(BF16)
    tail_x_out[2] = x1.astype(BF16)
    first = iota((1, 128), 1) < 64

    def per_head(ref):
        return jnp.where(first, ref[:, 0:1], ref[:, 1:2])

    dt_raw = jnp.concatenate(
        [jnp.where(first, raw[:, k : k + 1], raw[:, k + 1 : k + 2]) for k in (32, 96)], axis=0
    )
    step_size = jax.nn.softplus(dt_raw + per_head(dt_bias))
    decay = jnp.exp(-step_size * per_head(decay_rate))
    a = step_size * xc
    skip = per_head(skip_gain) * xc
    gate = jax.nn.silu(gate_raw)
    d0, d1 = decay[:16], decay[16:]
    d01 = d0 * d1
    a0, a1 = a[:16], a[16:]
    loads[4].wait()
    for r in range(16):
        sl[:, r * 128 : r * 128 + 128] = st[r].astype(BF16)

    arrived(ra.at[0:7], ssem.at[0])
    arrived(rb.at[0:7], ssem.at[1])
    arrived(wo.at[0, 0:384, :], wsend)
    arrived(rc, rsem.at[2])
    def channels(k):
        u = rc[k].astype(F32) + rc[k + 1].astype(F32)
        v = rc[k + 2].astype(F32) + rc[k + 3].astype(F32)
        return jnp.where(low, u, pltpu.roll(v, 64, 1)), jnp.where(low, pltpu.roll(u, 64, 1), v)

    b0, b1 = channels(0)
    c0, c1 = channels(4)
    c_low = jnp.concatenate([c0, c1], axis=0).astype(BF16)
    mod16 = iota((32, 128), 0) % 16
    zero_low = jnp.zeros((32, 128), BF16)
    spread = jnp.concatenate([jnp.where(mod16 == r, c_low, zero_low) for r in range(16)], axis=1)
    read = lax.dot_general(spread, sl[...], NT, preferred_element_type=F32)

    def along(u, v):
        return jnp.sum(u * v, axis=1, keepdims=True)

    y0 = d0 * read[:16] + a0 * along(b0, c0)
    y1 = d01 * read[16:] + d1 * a0 * along(b0, c1) + a1 * along(b1, c1)
    gated = (jnp.concatenate([y0, y1], axis=0) + skip) * gate
    gs[...] = gated
    s3[...] = jnp.zeros_like(s3)
    s3r = s3.reshape(64, 128)
    for k in range(8):
        p, t, u = k // 4, k // 2 % 2, k % 2
        s3r[pl.ds(k, 4, stride=16), :] = gs[pl.ds(t * 16 + p * 8 + u, 4, stride=2), :]
    gain_high = norm_gain[...].astype(BF16).astype(F32)
    s3r[pl.ds(8, 4, stride=16), :] = jnp.broadcast_to(gain_high, (4, 128))
    s3r[pl.ds(9, 4, stride=16), :] = jnp.broadcast_to(norm_gain[...] - gain_high, (4, 128))
    s3b[...] = s3[...].astype(BF16)

    for d in range(1, 4):
        to = lax.rem(place + d, 4)
        send(s3b.at[to], r3.at[place], ssem.at[3], rsem.at[3], (quad * 4 + to, row))
    r3[place] = s3b[place]

    def high_low(v):
        high = v.astype(BF16).astype(F32)
        return [high, (v - high).astype(BF16).astype(F32)]

    d10 = d1 * a0
    zero = jnp.zeros((16, 128), F32)
    columns = jnp.concatenate(
        high_low(d01) + high_low(d10) + high_low(a1) + [zero, zero], axis=0
    )
    columns = jnp.transpose(columns).astype(BF16)
    one = jnp.ones((16, 128), F32)
    left = jnp.concatenate([zero, zero, b0, b0, b1, b1, zero, zero], axis=0)
    right = jnp.concatenate([one, one, zero, zero, zero, zero, zero, zero], axis=0)
    both = jnp.concatenate([left, right], axis=1)
    which = iota((128, 256), 0) % 16

    def update(r):
        picked = jnp.where(which == r, both, 0.0).astype(BF16)
        made = dot(columns, picked)
        so[r] = st[r] * made[:, 128:] + made[:, :128]

    for r in range(8):
        update(r)

    arrived(r3.at[0:3], rsem.at[3])
    blocks = [r3[n].astype(F32) for n in range(4)]
    square = sum(v[0:8] * v[0:8] for v in blocks)
    square = jnp.broadcast_to(jnp.sum(square, axis=1, keepdims=True), (8, 128))
    rows = [v[0:8] * (v[8:9] + v[9:10]) for v in blocks] + [square, jnp.zeros((8, 128), F32)]
    r4[row] = jnp.concatenate(rows, axis=0).astype(BF16)
    for to in row_peers:
        send(r4.at[row], r4.at[row], ssem.at[4], rsem.at[4], (head, to))
    arrived(r3.at[0:3], ssem.at[3])

    arrived(wo.at[core], wrecv)
    sibling = head + 1 - 2 * core
    send(wo.at[core], wo.at[core], csend, crecv, (sibling, row))

    for r in range(8, 16):
        update(r)

    arrived(r4.at[0:7], rsem.at[4])
    f4[...] = r4[...].reshape(384, 128).astype(F32)
    which_row = lax.div(iota((8, 128), 1), 32)
    for p in range(2):
        square = f4[pl.ds(32 + p * 4, 8, stride=48), :]
        for n in range(1, 4):
            square = jnp.where(which_row == n, f4[pl.ds(32 + p * 4 + n, 8, stride=48), :], square)
        for i in range(8):
            sq[2 * i + p] = square[i : i + 1]
    for d in (4, 12, 3, 5, 11, 13, 2, 6, 10, 14, 1, 7, 9, 15, 8):
        to = lax.rem(quad + d, 16)
        send(sq.at[to], rq.at[quad], qsend, qrecv, (to * 4 + place, row))
    rq[quad] = sq[quad]
    for n in range(4):
        block = [f4[pl.ds(n * 8 + k, 8, stride=48), :] for k in range(8)]
        lhs[:, n * 128 : n * 128 + 128] = jnp.concatenate(block, axis=0).astype(BF16)
    arrived(wo.at[1 - core], crecv)
    f5r = f5.reshape(256, 128)
    for half in range(2):
        out = dot(lhs[...], wo[half])
        for n in range(8):
            for k in range(2):
                at = n // 4 * 16 + n % 4 * 4 + half * 2 + k
                f5r[pl.ds(at, 8, stride=32), :] = out[n * 8 : n * 8 + 8, k * 128 : k * 128 + 128]
    s5[...] = f5[...].astype(BF16)
    for d in (4, 12, 3, 5, 11, 13, 2, 6, 10, 14, 1, 7, 9, 15, 8):
        to = lax.rem(quad + d, 16)
        send(s5.at[to], r5.at[quad], xsend, xrecv, (to * 4 + place, row))
    r5[quad] = s5[quad]
    arrived(r4.at[0:7], ssem.at[4])
    arrived(wo.at[core], csend)

    @pl.when(grp == bc_group)
    def _():
        arrived(rc.at[0:7], ssem.at[2])

    @pl.when(grp != bc_group)
    def _():
        arrived(rc, ssem.at[2])

    arrived(r5.at[0:15], xsend)
    arrived(r5.at[0:15], xrecv)
    arrived(rq.at[0:15], qsend)
    arrived(rq.at[0:15], qrecv)
    parts[...] = r5[...]
    squares[...] = rq[...]


def hand_over(parts, squares, a, b, c, layer_out, oa, ob, oc, made, o5, sem):
    moves = [(a.at[4 * n : 4 * n + 4], oa.at[4 * n : 4 * n + 4]) for n in range(4)] + [(b, ob), (c, oc)]
    copies = [pltpu.make_async_copy(src, dst, sem.at[n]) for n, (src, dst) in enumerate(moves)]
    for copy in copies:
        copy.start()
    total = jnp.zeros((16, 128), F32)
    mine = lax.div(iota((16, 128), 0), 4) * 32 == iota((16, 128), 1)
    for i in range(8):
        both = parts[2 * i].astype(F32) + parts[2 * i + 1].astype(F32)
        scale = lax.rsqrt((squares[2 * i] + squares[2 * i + 1]) / 1024.0 + EPS)
        total += both * jnp.sum(jnp.where(mine, scale, 0.0), axis=1, keepdims=True)
    o5[...] = total
    for s in range(2):
        for k in range(4):
            pair = o5[pl.ds(s * 8 + k, 2, stride=4), :]
            made[s, :, k * 128 : k * 128 + 128] = pair.astype(BF16)
    last = pltpu.make_async_copy(made, layer_out, sem.at[6])
    last.start()
    for copy in copies:
        copy.wait()
    last.wait()


def local(
    tokens, w_zx, w_bc, w_dt, conv_wx, conv_bx, conv_wbc, conv_bbc,
    dt_bias, decay_rate, skip_gain, norm_gain, w_out, ssm_state, tail_x, tail_bc,
):
    hbm = pl.BlockSpec(memory_space=pltpu.HBM)
    vmem = pl.BlockSpec(memory_space=pltpu.VMEM)
    V = pltpu.VMEM
    dma = pltpu.SemaphoreType.DMA
    shapes = (
        jax.ShapeDtypeStruct((2, 2, 512), BF16),
        jax.ShapeDtypeStruct((16, 128, 128), F32),
        jax.ShapeDtypeStruct((3, 16, 128), BF16),
        jax.ShapeDtypeStruct((3, 16, 32), BF16),
    )
    operands = (
        tokens,
        w_zx.reshape(1024, 128),
        w_bc.T,
        w_dt.T,
        w_out,
        ssm_state.reshape(16, 128, 128),
        conv_wx,
        conv_bx.reshape(1, 128),
        conv_wbc,
        conv_bbc.reshape(1, 32),
        dt_bias.reshape(1, 2),
        decay_rate.reshape(1, 2),
        skip_gain.reshape(1, 2),
        norm_gain.reshape(1, 128),
        jnp.transpose(tail_x, (1, 0, 2)),
        jnp.transpose(tail_bc, (1, 0, 2)),
    )
    made = pl.pallas_call(
        kernel,
        out_shape=(V((16, 16, 128), BF16), V((16, 1, 128), F32), *(V(v.shape, v.dtype) for v in shapes[1:])),
        in_specs=[hbm] * 16,
        out_specs=(vmem,) * 5,
        scratch_shapes=[
            V((2, 128, 512), BF16),
            V((1024, 128), BF16),
            V((32, 512), BF16),
            V((2, 512), BF16),
            V((16, 128, 128), F32),
            V((4, 128), F32),
            V((1, 128), F32),
            V((4, 32), F32),
            V((1, 32), F32),
            V((1, 2), F32),
            V((1, 2), F32),
            V((1, 2), F32),
            V((1, 128), F32),
            V((3, 16, 128), BF16),
            V((3, 16, 32), BF16),
            V((1024, 128), F32),
            V((128, 512), BF16),
            V((512, 256), BF16),
            V((8, 16, 128), BF16),
            V((8, 16, 128), BF16),
            V((8, 2, 32, 128), BF16),
            V((8, 2, 32, 128), BF16),
            V((16, 128), BF16),
            V((8, 16, 128), BF16),
            V((4, 16, 128), F32),
            V((4, 16, 128), BF16),
            V((4, 16, 128), BF16),
            V((8, 48, 128), BF16),
            V((16, 16, 128), BF16),
            V((16, 16, 128), BF16),
            V((16, 1, 128), F32),
            V((16, 1, 128), F32),
            V((2, 512, 256), BF16),
            V((32, 128), F32),
            V((384, 128), F32),
            V((64, 512), BF16),
            V((16, 16, 128), F32),
            V((128, 2048), BF16),
            dma((15,)),
            dma((5,)),
            dma((5,)),
            dma,
            dma,
            dma,
            dma,
            pltpu.SemaphoreType.REGULAR,
            pltpu.SemaphoreType.REGULAR,
            dma,
            dma,
            dma,
            dma,
        ],
        compiler_params=pltpu.CompilerParams(
            collective_id=0, has_side_effects=True, vmem_limit_bytes=32 << 20
        ),
    )(*(pltpu.with_memory_space_constraint(v, pltpu.HBM) for v in operands))
    outs = pl.pallas_call(
        hand_over,
        out_shape=shapes,
        in_specs=[vmem, vmem] + [pl.BlockSpec(memory_space=pl.ANY)] * 3,
        out_specs=(hbm,) * 4,
        scratch_shapes=[V((2, 2, 512), BF16), V((16, 128), F32), dma((7,))],
        compiler_params=pltpu.CompilerParams(vmem_limit_bytes=32 << 20),
    )(*made)
    back = (1, 0, 2)
    return outs[0], outs[1].reshape(16, 2, 64, 128), jnp.transpose(outs[2], back), jnp.transpose(outs[3], back)


def solution(mesh):
    placed = (
        P(None, None, "row"),
        P("row", None, "head"),
        P("row", "head"),
        P("row", "head"),
        P(None, "head"),
        P("head"),
        P(None, "head"),
        P("head"),
        P("head"),
        P("head"),
        P("head"),
        P("head"),
        P("head", "row"),
        P("row", "head", None, None),
        P("row", None, "head"),
        P("row", None, "head"),
    )
    return jax.shard_map(
        local,
        mesh=mesh,
        in_specs=placed,
        out_specs=(
            P(None, "head", "row"),
            P("row", "head", None, None),
            P("row", None, "head"),
            P("row", None, "head"),
        ),
        check_vma=False,
    )
```

```python
import jax
import jax.numpy as jnp
from jax import lax
from jax.experimental import pallas as pl
from jax.experimental.pallas import tpu as pltpu
from jax.sharding import PartitionSpec as P

MESH = pl.DeviceIdType.MESH
F32 = jnp.float32
BF16 = jnp.bfloat16
EPS = 1e-05
NT = (((1,), (1,)), ((), ()))


def dot(a, b):
    return jnp.dot(a, b, preferred_element_type=F32)


def iota(shape, dim):
    return lax.broadcasted_iota(jnp.int32, shape, dim)


def kernel(
    tokens_h, w_zx_h, w_bc_h, w_dt_h, w_out, state_h,
    conv_wx_h, conv_bx_h, conv_wbc_h, conv_bbc_h, dt_bias_h, decay_rate_h, skip_gain_h, norm_gain_h, tail_x_h, tail_bc_h,
    parts, squares, so, tail_x_out, tail_bc_out,
    tok, wz, wbc, wdt, st, conv_wx, conv_bx, conv_wbc, conv_bbc, dt_bias, decay_rate, skip_gain, norm_gain, tail_x, tail_bc,
    zf, wa, wgx,
    sa, ra, sb, rb, sc, rc, s3, s3b, r3, r4, s5, r5, sq, rq, wo,
    gs, f5, sl,
    lsem, ssem, rsem, wsend, wrecv, csend, crecv, near, far, xsend, xrecv, qsend, qrecv, rowsem,
):
    row = lax.axis_index("row")
    head = lax.axis_index("head")
    grp = lax.div(head, 8)
    mem = lax.rem(head, 8)
    quad = lax.div(head, 4)
    place = lax.rem(head, 4)
    core = lax.rem(head, 2)
    owner_kind = lax.div(head, 32)
    bc_group = lax.div(lax.rem(head, 32), 4)

    sources = (
        tokens_h, w_bc_h, w_dt_h, w_zx_h, state_h, conv_wbc_h, conv_bbc_h, tail_bc_h,
        conv_wx_h, conv_bx_h, dt_bias_h, decay_rate_h, skip_gain_h, norm_gain_h, tail_x_h,
    )
    targets = (
        tok, wbc, wdt, wz, st, conv_wbc, conv_bbc, tail_bc,
        conv_wx, conv_bx, dt_bias, decay_rate, skip_gain, norm_gain, tail_x,
    )
    loads = [pltpu.make_async_copy(a, b, lsem.at[n]) for n, (a, b) in enumerate(zip(sources, targets))]
    for load in loads[:3]:
        load.start()

    barrier = pltpu.get_barrier_semaphore()

    def signal(sem, h, r):
        pl.semaphore_signal(sem, inc=1, device_id=(h, r), device_id_type=MESH)

    def row_peer(dy, dx):
        return lax.rem(row - x_hi + 2 * dy, 8) + lax.rem(x_hi + dx, 2)

    x_hi = lax.rem(row, 2)
    row_peers = [row_peer(dy, dx) for dy, dx in ((2, 1), (1, 1), (3, 1), (2, 0), (0, 1), (1, 0), (3, 0))]
    chip = head - core
    for peer in row_peers:
        signal(barrier, chip, peer)
    other = quad * 4 + lax.rem(place - core + 2, 4)
    signal(barrier, other, row)

    @pl.when(core == 1)
    def _():
        signal(barrier, chip, row)

    for load in loads[3:]:
        load.start()
    for d in range(1, 16):
        signal(barrier, lax.rem(chip + 4 * d, 64) + 1, row)
    for n in range(4):
        src = (n // 2) * 32 + grp * 4 + (n % 2) * 2

        @pl.when(src != chip)
        def _():
            signal(barrier, src + 1, row)

    loads[1].wait()
    loads[2].wait()
    steps = jnp.concatenate([wdt[...].astype(F32), jnp.zeros((30, 512), F32)], axis=0).astype(BF16)
    for n in range(2):
        wa[n * 64 : n * 64 + 32, :] = wbc[...]
        wa[n * 64 + 32 : n * 64 + 64, :] = steps
    loads[0].wait()
    toks = tok[...].reshape(256, 512)
    pa = lax.dot_general(toks, wa[...], NT, preferred_element_type=F32)
    pa = jnp.where(iota((128, 128), 1) < 64, pa[:128], pa[128:]).astype(BF16)
    for i in range(8):
        sa[i] = pa[i * 16 : i * 16 + 16]

    @pl.when(core == 0)
    def _():
        pl.semaphore_wait(barrier, 17)
        signal(near, head + 1, row)

    @pl.when(core == 1)
    def _():
        pl.semaphore_wait(near, 1)


    def send(src, dst, ss, rs, device):
        copy = pltpu.make_async_remote_copy(
            src_ref=src, dst_ref=dst, send_sem=ss, recv_sem=rs, device_id=device, device_id_type=MESH
        )
        copy.start()
        return copy

    for to in row_peers:
        send(sa.at[to], ra.at[row], ssem.at[0], rsem.at[0], (head, to))

    loads[3].wait()
    zf[...] = wz[...].astype(F32)
    wgx[:, :128] = zf[pl.ds(0, 512, stride=2), :].astype(BF16)
    wgx[:, 128:] = zf[pl.ds(1, 512, stride=2), :].astype(BF16)
    pz = dot(toks, wgx[...])
    for i in range(8):
        for s in range(2):
            piece = pz[s * 128 + i * 16 : s * 128 + i * 16 + 16, :].astype(BF16)
            sb[i, 0, s * 16 : s * 16 + 16, :] = piece[:, :128]
            sb[i, 1, s * 16 : s * 16 + 16, :] = piece[:, 128:]
    for to in row_peers:
        send(sb.at[to], rb.at[row], ssem.at[1], rsem.at[1], (head, to))

    for n in range(4):
        part = w_out.at[:, (n % 2) * 256 : (n % 2) * 256 + 256]
        spot = wo.at[n % 2, pl.ds(place * 128, 128), :]

        @pl.when(place != n)
        def _():
            send(part, spot, wsend, wrecv, (quad * 4 + n, row))

        @pl.when(place == n)
        def _():
            pltpu.make_async_copy(part, spot, wrecv).start()

    ra[row] = sa[row]
    rb[row] = sb[row]

    for n in range(5, 15):
        loads[n].wait()

    def taps(window, weight, bias):
        summed = bias
        for k in range(4):
            summed = summed + window[k] * weight[k : k + 1, :]
        return jax.nn.silu(summed).astype(BF16).astype(F32)

    old_bc = [jnp.concatenate([tail_bc[k].astype(F32)] * 4, axis=1) for k in range(3)]
    old_x = [tail_x[k].astype(F32) for k in range(3)]
    weight_bc = jnp.concatenate([conv_wbc[...]] * 4, axis=1)
    bias_bc = jnp.concatenate([conv_bbc[...]] * 4, axis=1)

    def arrived(buf, sem):
        pltpu.make_async_copy(buf, buf, sem).wait()

    arrived(ra.at[0:7], rsem.at[0])
    total = ra[0].astype(F32)
    for i in range(1, 8):
        total += ra[i].astype(F32)
    raw = total.astype(BF16).astype(F32)
    lane = iota((16, 128), 1)
    low = lane < 64
    raw_bc = jnp.where(lane % 64 < 32, raw, pltpu.roll(raw, 32, 1))
    window = (
        jnp.where(low, old_bc[0], old_bc[1]),
        jnp.where(low, old_bc[1], old_bc[2]),
        jnp.where(low, old_bc[2], pltpu.roll(raw_bc, 64, 1)),
        raw_bc,
    )
    conv_bc = taps(window, weight_bc, bias_bc)
    sc[...] = jnp.where(lax.rem(lax.div(lane, 32), 2) == lax.rem(place, 2), conv_bc, 0.0).astype(BF16)

    @pl.when(core == 1)
    def _():
        pl.semaphore_wait(barrier, jnp.where(grp == bc_group, 36, 38))
        signal(far, head - 1, row)

    @pl.when(core == 0)
    def _():
        pl.semaphore_wait(far, 1)

    slot = owner_kind * 4 + place
    for n in range(8):
        to = bc_group * 8 + n

        @pl.when(to != head)
        def _():
            send(sc, rc.at[slot], ssem.at[2], rsem.at[2], (to, row))

        @pl.when(to == head)
        def _():
            pltpu.make_async_copy(sc, rc.at[slot], rsem.at[2]).start()

    tail_bc_out[0] = tail_bc[2]
    tail_bc_out[1] = raw[:, :32].astype(BF16)
    tail_bc_out[2] = pltpu.roll(raw, 64, 1)[:, :32].astype(BF16)

    arrived(rb.at[0:7], rsem.at[1])
    mixed = []
    for part in range(2):
        total = rb[0, part].astype(F32)
        for i in range(1, 8):
            total += rb[i, part].astype(F32)
        mixed.append(total.astype(BF16).astype(F32))
    gate_raw, raw_x = mixed
    x0, x1 = raw_x[:16], raw_x[16:]
    xc0 = taps((old_x[0], old_x[1], old_x[2], x0), conv_wx[...], conv_bx[...])
    xc1 = taps((old_x[1], old_x[2], x0, x1), conv_wx[...], conv_bx[...])
    xc = jnp.concatenate([xc0, xc1], axis=0)
    tail_x_out[0] = tail_x[2]
    tail_x_out[1] = x0.astype(BF16)
    tail_x_out[2] = x1.astype(BF16)
    first = iota((1, 128), 1) < 64

    def per_head(ref):
        return jnp.where(first, ref[:, 0:1], ref[:, 1:2])

    dt_raw = jnp.concatenate(
        [jnp.where(first, raw[:, k : k + 1], raw[:, k + 1 : k + 2]) for k in (32, 96)], axis=0
    )
    step_size = jax.nn.softplus(dt_raw + per_head(dt_bias))
    decay = jnp.exp(-step_size * per_head(decay_rate))
    a = step_size * xc
    skip = per_head(skip_gain) * xc
    gate = jax.nn.silu(gate_raw)
    d0, d1 = decay[:16], decay[16:]
    d01 = d0 * d1
    a0, a1 = a[:16], a[16:]
    loads[4].wait()
    for r in range(16):
        sl[:, r * 128 : r * 128 + 128] = st[r].astype(BF16)

    arrived(ra.at[0:7], ssem.at[0])
    arrived(rb.at[0:7], ssem.at[1])
    arrived(wo.at[0, 0:384, :], wsend)
    arrived(rc, rsem.at[2])
    def channels(k):
        u = rc[k].astype(F32) + rc[k + 1].astype(F32)
        v = rc[k + 2].astype(F32) + rc[k + 3].astype(F32)
        return jnp.where(low, u, pltpu.roll(v, 64, 1)), jnp.where(low, pltpu.roll(u, 64, 1), v)

    b0, b1 = channels(0)
    c0, c1 = channels(4)
    c_low = jnp.concatenate([c0, c1], axis=0).astype(BF16)
    mod16 = iota((32, 128), 0) % 16
    zero_low = jnp.zeros((32, 128), BF16)
    spread = jnp.concatenate([jnp.where(mod16 == r, c_low, zero_low) for r in range(16)], axis=1)
    read = lax.dot_general(spread, sl[...], NT, preferred_element_type=F32)

    def along(u, v):
        return jnp.sum(u * v, axis=1, keepdims=True)

    y0 = d0 * read[:16] + a0 * along(b0, c0)
    y1 = d01 * read[16:] + d1 * a0 * along(b0, c1) + a1 * along(b1, c1)
    gated = (jnp.concatenate([y0, y1], axis=0) + skip) * gate
    gs[...] = gated
    s3[...] = jnp.zeros_like(s3)
    s3r = s3.reshape(64, 128)
    for k in range(8):
        p, t, u = k // 4, k // 2 % 2, k % 2
        s3r[pl.ds(k, 4, stride=16), :] = gs[pl.ds(t * 16 + p * 8 + u, 4, stride=2), :]
    gain_high = norm_gain[...].astype(BF16).astype(F32)
    s3r[pl.ds(8, 4, stride=16), :] = jnp.broadcast_to(gain_high, (4, 128))
    s3r[pl.ds(9, 4, stride=16), :] = jnp.broadcast_to(norm_gain[...] - gain_high, (4, 128))
    s3b[...] = s3[...].astype(BF16)

    for d in range(1, 4):
        to = lax.rem(place + d, 4)
        send(s3b.at[to], r3.at[place], ssem.at[3], rsem.at[3], (quad * 4 + to, row))
    r3[place] = s3b[place]

    arrived(wo.at[core], wrecv)
    sibling = head + 1 - 2 * core
    send(wo.at[core], wo.at[core], csend, crecv, (sibling, row))

    def high_low(v):
        high = v.astype(BF16).astype(F32)
        return [high, (v - high).astype(BF16).astype(F32)]

    d10 = d1 * a0
    zero = jnp.zeros((16, 128), F32)
    columns = jnp.concatenate(
        high_low(d01) + high_low(d10) + high_low(a1) + [zero, zero], axis=0
    )
    columns = jnp.transpose(columns).astype(BF16)
    one = jnp.ones((16, 128), F32)
    left = jnp.concatenate([zero, zero, b0, b0, b1, b1, zero, zero], axis=0)
    right = jnp.concatenate([one, one, zero, zero, zero, zero, zero, zero], axis=0)
    both = jnp.concatenate([left, right], axis=1)
    which = iota((128, 256), 0) % 16

    def update(r):
        picked = jnp.where(which == r, both, 0.0).astype(BF16)
        made = dot(columns, picked)
        so[r] = st[r] * made[:, 128:] + made[:, :128]

    for r in range(8):
        update(r)

    arrived(r3.at[0:3], rsem.at[3])
    blocks = [r3[n].astype(F32) for n in range(4)]
    square = sum(v[0:8] * v[0:8] for v in blocks)
    square = jnp.broadcast_to(jnp.sum(square, axis=1, keepdims=True), (8, 128))
    rows = [v[0:8] * (v[8:9] + v[9:10]) for v in blocks] + [square, jnp.zeros((8, 128), F32)]
    r4[row] = jnp.concatenate(rows, axis=0).astype(BF16)
    for to in row_peers:
        send(r4.at[row], r4.at[row], ssem.at[4], rowsem.at[row], (head, to))
    arrived(r3.at[0:3], ssem.at[3])

    which_row = lax.div(iota((1, 128), 1), 32)
    arrived(wo.at[1 - core], crecv)

    def onward(peers):
        rows = []
        for peer in peers:
            block = r4[peer].astype(F32)
            rows.append(jnp.concatenate([block[n * 8 : n * 8 + 8] for n in range(4)], axis=1))
            for p in range(2):
                square = block[32 + p * 4 : 33 + p * 4]
                for n in range(1, 4):
                    square = jnp.where(which_row == n, block[32 + p * 4 + n : 33 + p * 4 + n], square)
                sq[2 * peer + p] = square
        left_side = jnp.concatenate(rows, axis=0).astype(BF16)
        outs = [dot(left_side, wo[n]) for n in range(2)]
        for b, peer in enumerate(peers):
            for p in range(2):
                to = 2 * peer + p
                for k in range(4):
                    at = b * 8 + p * 4
                    f5[to, pl.ds(k, 4, stride=4), :] = outs[k // 2][at : at + 4, k % 2 * 128 : k % 2 * 128 + 128]
                s5[to] = f5[to].astype(BF16)

                @pl.when(to != quad)
                def _():
                    send(sq.at[to], rq.at[quad], qsend, qrecv, (to * 4 + place, row))
                    send(s5.at[to], r5.at[quad], xsend, xrecv, (to * 4 + place, row))

    onward([row])
    for r in range(8, 16):
        update(r)
    for peers in (row_peers[5:7], row_peers[3:5], row_peers[1:3], row_peers[0:1]):
        for peer in peers:
            arrived(r4.at[peer], rowsem.at[peer])
        onward(peers)
    rq[quad] = sq[quad]
    r5[quad] = s5[quad]
    arrived(r4.at[0:7], ssem.at[4])
    arrived(wo.at[core], csend)

    @pl.when(grp == bc_group)
    def _():
        arrived(rc.at[0:7], ssem.at[2])

    @pl.when(grp != bc_group)
    def _():
        arrived(rc, ssem.at[2])

    arrived(r5.at[0:15], xsend)
    arrived(r5.at[0:15], xrecv)
    arrived(rq.at[0:15], qsend)
    arrived(rq.at[0:15], qrecv)
    parts[...] = r5[...]
    squares[...] = rq[...]


def hand_over(parts, squares, a, b, c, layer_out, oa, ob, oc, made, o5, sem):
    moves = [(a.at[4 * n : 4 * n + 4], oa.at[4 * n : 4 * n + 4]) for n in range(4)] + [(b, ob), (c, oc)]
    copies = [pltpu.make_async_copy(src, dst, sem.at[n]) for n, (src, dst) in enumerate(moves)]
    for copy in copies:
        copy.start()
    total = jnp.zeros((16, 128), F32)
    mine = lax.div(iota((16, 128), 0), 4) * 32 == iota((16, 128), 1)
    for i in range(8):
        both = parts[2 * i].astype(F32) + parts[2 * i + 1].astype(F32)
        scale = lax.rsqrt((squares[2 * i] + squares[2 * i + 1]) / 1024.0 + EPS)
        total += both * jnp.sum(jnp.where(mine, scale, 0.0), axis=1, keepdims=True)
    o5[...] = total
    for s in range(2):
        for k in range(4):
            pair = o5[pl.ds(s * 8 + k, 2, stride=4), :]
            made[s, :, k * 128 : k * 128 + 128] = pair.astype(BF16)
    last = pltpu.make_async_copy(made, layer_out, sem.at[6])
    last.start()
    for copy in copies:
        copy.wait()
    last.wait()


def local(
    tokens, w_zx, w_bc, w_dt, conv_wx, conv_bx, conv_wbc, conv_bbc,
    dt_bias, decay_rate, skip_gain, norm_gain, w_out, ssm_state, tail_x, tail_bc,
):
    hbm = pl.BlockSpec(memory_space=pltpu.HBM)
    vmem = pl.BlockSpec(memory_space=pltpu.VMEM)
    V = pltpu.VMEM
    dma = pltpu.SemaphoreType.DMA
    shapes = (
        jax.ShapeDtypeStruct((2, 2, 512), BF16),
        jax.ShapeDtypeStruct((16, 128, 128), F32),
        jax.ShapeDtypeStruct((3, 16, 128), BF16),
        jax.ShapeDtypeStruct((3, 16, 32), BF16),
    )
    operands = (
        tokens,
        w_zx.reshape(1024, 128),
        w_bc.T,
        w_dt.T,
        w_out,
        ssm_state.reshape(16, 128, 128),
        conv_wx,
        conv_bx.reshape(1, 128),
        conv_wbc,
        conv_bbc.reshape(1, 32),
        dt_bias.reshape(1, 2),
        decay_rate.reshape(1, 2),
        skip_gain.reshape(1, 2),
        norm_gain.reshape(1, 128),
        jnp.transpose(tail_x, (1, 0, 2)),
        jnp.transpose(tail_bc, (1, 0, 2)),
    )
    made = pl.pallas_call(
        kernel,
        out_shape=(V((16, 16, 128), BF16), V((16, 1, 128), F32), *(V(v.shape, v.dtype) for v in shapes[1:])),
        in_specs=[hbm] * 16,
        out_specs=(vmem,) * 5,
        scratch_shapes=[
            V((2, 128, 512), BF16),
            V((1024, 128), BF16),
            V((32, 512), BF16),
            V((2, 512), BF16),
            V((16, 128, 128), F32),
            V((4, 128), F32),
            V((1, 128), F32),
            V((4, 32), F32),
            V((1, 32), F32),
            V((1, 2), F32),
            V((1, 2), F32),
            V((1, 2), F32),
            V((1, 128), F32),
            V((3, 16, 128), BF16),
            V((3, 16, 32), BF16),
            V((1024, 128), F32),
            V((128, 512), BF16),
            V((512, 256), BF16),
            V((8, 16, 128), BF16),
            V((8, 16, 128), BF16),
            V((8, 2, 32, 128), BF16),
            V((8, 2, 32, 128), BF16),
            V((16, 128), BF16),
            V((8, 16, 128), BF16),
            V((4, 16, 128), F32),
            V((4, 16, 128), BF16),
            V((4, 16, 128), BF16),
            V((8, 48, 128), BF16),
            V((16, 16, 128), BF16),
            V((16, 16, 128), BF16),
            V((16, 1, 128), F32),
            V((16, 1, 128), F32),
            V((2, 512, 256), BF16),
            V((32, 128), F32),
            V((16, 16, 128), F32),
            V((128, 2048), BF16),
            dma((15,)),
            dma((5,)),
            dma((5,)),
            dma,
            dma,
            dma,
            dma,
            pltpu.SemaphoreType.REGULAR,
            pltpu.SemaphoreType.REGULAR,
            dma,
            dma,
            dma,
            dma,
            dma((8,)),
        ],
        compiler_params=pltpu.CompilerParams(
            collective_id=0, has_side_effects=True, vmem_limit_bytes=32 << 20
        ),
    )(*(pltpu.with_memory_space_constraint(v, pltpu.HBM) for v in operands))
    outs = pl.pallas_call(
        hand_over,
        out_shape=shapes,
        in_specs=[vmem, vmem] + [pl.BlockSpec(memory_space=pl.ANY)] * 3,
        out_specs=(hbm,) * 4,
        scratch_shapes=[V((2, 2, 512), BF16), V((16, 128), F32), dma((7,))],
        compiler_params=pltpu.CompilerParams(vmem_limit_bytes=32 << 20),
    )(*made)
    back = (1, 0, 2)
    return outs[0], outs[1].reshape(16, 2, 64, 128), jnp.transpose(outs[2], back), jnp.transpose(outs[3], back)


def solution(mesh):
    placed = (
        P(None, None, "row"),
        P("row", None, "head"),
        P("row", "head"),
        P("row", "head"),
        P(None, "head"),
        P("head"),
        P(None, "head"),
        P("head"),
        P("head"),
        P("head"),
        P("head"),
        P("head"),
        P("head", "row"),
        P("row", "head", None, None),
        P("row", None, "head"),
        P("row", None, "head"),
    )
    return jax.shard_map(
        local,
        mesh=mesh,
        in_specs=placed,
        out_specs=(
            P(None, "head", "row"),
            P("row", "head", None, None),
            P("row", None, "head"),
            P("row", None, "head"),
        ),
        check_vma=False,
    )
```

```python
import jax
import jax.numpy as jnp
from jax import lax
from jax.experimental import pallas as pl
from jax.experimental.pallas import tpu as pltpu
from jax.sharding import PartitionSpec as P

MESH = pl.DeviceIdType.MESH
F32 = jnp.float32
BF16 = jnp.bfloat16
EPS = 1e-05
NT = (((1,), (1,)), ((), ()))


def dot(a, b):
    return jnp.dot(a, b, preferred_element_type=F32)


def iota(shape, dim):
    return lax.broadcasted_iota(jnp.int32, shape, dim)


def kernel(
    tokens_h, w_zx_h, w_bc_h, w_dt_h, w_out, state_h,
    conv_wx_h, conv_bx_h, conv_wbc_h, conv_bbc_h, dt_bias_h, decay_rate_h, skip_gain_h, norm_gain_h, tail_x_h, tail_bc_h,
    parts, squares, so, tail_x_out, tail_bc_out,
    tok, wz, wbc, wdt, st, conv_wx, conv_bx, conv_wbc, conv_bbc, dt_bias, decay_rate, skip_gain, norm_gain, tail_x, tail_bc,
    zf, wa, wgx,
    sa, ra, sb, rb, sc, rc, s3, s3b, r3, r4, s5, r5, sq, rq, wo,
    gs, f5, sl,
    lsem, ssem, rsem, wsend, wrecv, csend, crecv, near, far, xsend, xrecv, qsend, qrecv, rowsem,
):
    row = lax.axis_index("row")
    head = lax.axis_index("head")
    grp = lax.div(head, 8)
    mem = lax.rem(head, 8)
    quad = lax.div(head, 4)
    place = lax.rem(head, 4)
    core = lax.rem(head, 2)
    owner_kind = lax.div(head, 32)
    bc_group = lax.div(lax.rem(head, 32), 4)

    sources = (
        tokens_h, w_bc_h, w_dt_h, w_zx_h, state_h, conv_wbc_h, conv_bbc_h, tail_bc_h,
        conv_wx_h, conv_bx_h, dt_bias_h, decay_rate_h, skip_gain_h, norm_gain_h, tail_x_h,
    )
    targets = (
        tok, wbc, wdt, wz, st, conv_wbc, conv_bbc, tail_bc,
        conv_wx, conv_bx, dt_bias, decay_rate, skip_gain, norm_gain, tail_x,
    )
    loads = [pltpu.make_async_copy(a, b, lsem.at[n]) for n, (a, b) in enumerate(zip(sources, targets))]
    for load in loads[:3]:
        load.start()

    barrier = pltpu.get_barrier_semaphore()

    def signal(sem, h, r):
        pl.semaphore_signal(sem, inc=1, device_id=(h, r), device_id_type=MESH)

    def row_peer(dy, dx):
        return lax.rem(row - x_hi + 2 * dy, 8) + lax.rem(x_hi + dx, 2)

    x_hi = lax.rem(row, 2)
    row_peers = [row_peer(dy, dx) for dy, dx in ((2, 1), (1, 1), (3, 1), (2, 0), (0, 1), (1, 0), (3, 0))]
    chip = head - core
    for peer in row_peers:
        signal(barrier, chip, peer)
    other = quad * 4 + lax.rem(place - core + 2, 4)
    signal(barrier, other, row)

    @pl.when(core == 1)
    def _():
        signal(barrier, chip, row)

    for load in loads[3:]:
        load.start()
    for d in range(1, 16):
        signal(barrier, lax.rem(chip + 4 * d, 64) + 1, row)
    for n in range(4):
        src = (n // 2) * 32 + grp * 4 + (n % 2) * 2

        @pl.when(src != chip)
        def _():
            signal(barrier, src + 1, row)

    loads[1].wait()
    loads[2].wait()
    steps = jnp.concatenate([wdt[...].astype(F32), jnp.zeros((30, 512), F32)], axis=0).astype(BF16)
    for n in range(2):
        wa[n * 64 : n * 64 + 32, :] = wbc[...]
        wa[n * 64 + 32 : n * 64 + 64, :] = steps
    loads[0].wait()
    toks = tok[...].reshape(256, 512)
    pa = lax.dot_general(toks, wa[...], NT, preferred_element_type=F32)
    pa = jnp.where(iota((128, 128), 1) < 64, pa[:128], pa[128:]).astype(BF16)
    for i in range(8):
        sa[i] = pa[i * 16 : i * 16 + 16]

    @pl.when(core == 0)
    def _():
        pl.semaphore_wait(barrier, 17)
        signal(near, head + 1, row)

    @pl.when(core == 1)
    def _():
        pl.semaphore_wait(near, 1)


    def send(src, dst, ss, rs, device):
        copy = pltpu.make_async_remote_copy(
            src_ref=src, dst_ref=dst, send_sem=ss, recv_sem=rs, device_id=device, device_id_type=MESH
        )
        copy.start()
        return copy

    for to in row_peers:
        send(sa.at[to], ra.at[row], ssem.at[0], rsem.at[0], (head, to))

    loads[3].wait()
    zf[...] = wz[...].astype(F32)
    wgx[:, :128] = zf[pl.ds(0, 512, stride=2), :].astype(BF16)
    wgx[:, 128:] = zf[pl.ds(1, 512, stride=2), :].astype(BF16)
    pz = dot(toks, wgx[...])
    for i in range(8):
        for s in range(2):
            piece = pz[s * 128 + i * 16 : s * 128 + i * 16 + 16, :].astype(BF16)
            sb[i, 0, s * 16 : s * 16 + 16, :] = piece[:, :128]
            sb[i, 1, s * 16 : s * 16 + 16, :] = piece[:, 128:]
    for to in row_peers:
        send(sb.at[to], rb.at[row], ssem.at[1], rsem.at[1], (head, to))

    for n in range(4):
        part = w_out.at[:, (n % 2) * 256 : (n % 2) * 256 + 256]
        spot = wo.at[n % 2, pl.ds(place * 128, 128), :]

        @pl.when(place != n)
        def _():
            send(part, spot, wsend, wrecv, (quad * 4 + n, row))

        @pl.when(place == n)
        def _():
            pltpu.make_async_copy(part, spot, wrecv).start()

    ra[row] = sa[row]
    rb[row] = sb[row]

    for n in range(5, 15):
        loads[n].wait()

    def taps(window, weight, bias):
        summed = bias
        for k in range(4):
            summed = summed + window[k] * weight[k : k + 1, :]
        return jax.nn.silu(summed).astype(BF16).astype(F32)

    old_bc = [jnp.concatenate([tail_bc[k].astype(F32)] * 4, axis=1) for k in range(3)]
    old_x = [tail_x[k].astype(F32) for k in range(3)]
    weight_bc = jnp.concatenate([conv_wbc[...]] * 4, axis=1)
    bias_bc = jnp.concatenate([conv_bbc[...]] * 4, axis=1)

    def arrived(buf, sem):
        pltpu.make_async_copy(buf, buf, sem).wait()

    arrived(ra.at[0:7], rsem.at[0])
    total = ra[0].astype(F32)
    for i in range(1, 8):
        total += ra[i].astype(F32)
    raw = total.astype(BF16).astype(F32)
    lane = iota((16, 128), 1)
    low = lane < 64
    raw_bc = jnp.where(lane % 64 < 32, raw, pltpu.roll(raw, 32, 1))
    window = (
        jnp.where(low, old_bc[0], old_bc[1]),
        jnp.where(low, old_bc[1], old_bc[2]),
        jnp.where(low, old_bc[2], pltpu.roll(raw_bc, 64, 1)),
        raw_bc,
    )
    conv_bc = taps(window, weight_bc, bias_bc)
    sc[...] = jnp.where(lax.rem(lax.div(lane, 32), 2) == lax.rem(place, 2), conv_bc, 0.0).astype(BF16)

    @pl.when(core == 1)
    def _():
        pl.semaphore_wait(barrier, jnp.where(grp == bc_group, 36, 38))
        signal(far, head - 1, row)

    @pl.when(core == 0)
    def _():
        pl.semaphore_wait(far, 1)

    slot = owner_kind * 4 + place
    for n in range(8):
        to = bc_group * 8 + n

        @pl.when(to != head)
        def _():
            send(sc, rc.at[slot], ssem.at[2], rsem.at[2], (to, row))

        @pl.when(to == head)
        def _():
            pltpu.make_async_copy(sc, rc.at[slot], rsem.at[2]).start()

    tail_bc_out[0] = tail_bc[2]
    tail_bc_out[1] = raw[:, :32].astype(BF16)
    tail_bc_out[2] = pltpu.roll(raw, 64, 1)[:, :32].astype(BF16)

    arrived(rb.at[0:7], rsem.at[1])
    mixed = []
    for part in range(2):
        total = rb[0, part].astype(F32)
        for i in range(1, 8):
            total += rb[i, part].astype(F32)
        mixed.append(total.astype(BF16).astype(F32))
    gate_raw, raw_x = mixed
    x0, x1 = raw_x[:16], raw_x[16:]
    xc0 = taps((old_x[0], old_x[1], old_x[2], x0), conv_wx[...], conv_bx[...])
    xc1 = taps((old_x[1], old_x[2], x0, x1), conv_wx[...], conv_bx[...])
    xc = jnp.concatenate([xc0, xc1], axis=0)
    tail_x_out[0] = tail_x[2]
    tail_x_out[1] = x0.astype(BF16)
    tail_x_out[2] = x1.astype(BF16)
    first = iota((1, 128), 1) < 64

    def per_head(ref):
        return jnp.where(first, ref[:, 0:1], ref[:, 1:2])

    dt_raw = jnp.concatenate(
        [jnp.where(first, raw[:, k : k + 1], raw[:, k + 1 : k + 2]) for k in (32, 96)], axis=0
    )
    step_size = jax.nn.softplus(dt_raw + per_head(dt_bias))
    decay = jnp.exp(-step_size * per_head(decay_rate))
    a = step_size * xc
    skip = per_head(skip_gain) * xc
    gate = jax.nn.silu(gate_raw)
    d0, d1 = decay[:16], decay[16:]
    d01 = d0 * d1
    a0, a1 = a[:16], a[16:]
    loads[4].wait()
    for r in range(16):
        sl[:, r * 128 : r * 128 + 128] = st[r].astype(BF16)

    arrived(ra.at[0:7], ssem.at[0])
    arrived(rb.at[0:7], ssem.at[1])
    arrived(wo.at[0, 0:384, :], wsend)
    s3[...] = jnp.zeros_like(s3)
    s3r = s3.reshape(64, 128)
    gain_high = norm_gain[...].astype(BF16).astype(F32)
    s3r[pl.ds(8, 4, stride=16), :] = jnp.broadcast_to(gain_high, (4, 128))
    s3r[pl.ds(9, 4, stride=16), :] = jnp.broadcast_to(norm_gain[...] - gain_high, (4, 128))
    arrived(rc, rsem.at[2])
    def channels(k):
        u = rc[k].astype(F32) + rc[k + 1].astype(F32)
        v = rc[k + 2].astype(F32) + rc[k + 3].astype(F32)
        return jnp.where(low, u, pltpu.roll(v, 64, 1)), jnp.where(low, pltpu.roll(u, 64, 1), v)

    b0, b1 = channels(0)
    c0, c1 = channels(4)
    c_low = jnp.concatenate([c0, c1], axis=0).astype(BF16)
    mod16 = iota((32, 128), 0) % 16
    zero_low = jnp.zeros((32, 128), BF16)
    spread = jnp.concatenate([jnp.where(mod16 == r, c_low, zero_low) for r in range(16)], axis=1)
    read = lax.dot_general(spread, sl[...], NT, preferred_element_type=F32)

    def along(u, v):
        return jnp.sum(u * v, axis=1, keepdims=True)

    y0 = d0 * read[:16] + a0 * along(b0, c0)
    y1 = d01 * read[16:] + d1 * a0 * along(b0, c1) + a1 * along(b1, c1)
    gated = (jnp.concatenate([y0, y1], axis=0) + skip) * gate
    gs[...] = gated
    for k in range(8):
        p, t, u = k // 4, k // 2 % 2, k % 2
        s3r[pl.ds(k, 4, stride=16), :] = gs[pl.ds(t * 16 + p * 8 + u, 4, stride=2), :]
    s3b[...] = s3[...].astype(BF16)

    for d in range(1, 4):
        to = lax.rem(place + d, 4)
        send(s3b.at[to], r3.at[place], ssem.at[3], rsem.at[3], (quad * 4 + to, row))
    r3[place] = s3b[place]

    arrived(wo.at[core], wrecv)
    sibling = head + 1 - 2 * core
    send(wo.at[core], wo.at[core], csend, crecv, (sibling, row))

    def high_low(v):
        high = v.astype(BF16).astype(F32)
        return [high, (v - high).astype(BF16).astype(F32)]

    d10 = d1 * a0
    zero = jnp.zeros((16, 128), F32)
    columns = jnp.concatenate(
        high_low(d01) + high_low(d10) + high_low(a1) + [zero, zero], axis=0
    )
    columns = jnp.transpose(columns).astype(BF16)
    one = jnp.ones((16, 128), F32)
    left = jnp.concatenate([zero, zero, b0, b0, b1, b1, zero, zero], axis=0)
    right = jnp.concatenate([one, one, zero, zero, zero, zero, zero, zero], axis=0)
    both = jnp.concatenate([left, right], axis=1)
    which = iota((128, 256), 0) % 16

    def update(r):
        picked = jnp.where(which == r, both, 0.0).astype(BF16)
        made = dot(columns, picked)
        so[r] = st[r] * made[:, 128:] + made[:, :128]

    for r in range(8):
        update(r)

    arrived(r3.at[0:3], rsem.at[3])
    blocks = [r3[n].astype(F32) for n in range(4)]
    square = sum(v[0:8] * v[0:8] for v in blocks)
    square = jnp.broadcast_to(jnp.sum(square, axis=1, keepdims=True), (8, 128))
    rows = [v[0:8] * (v[8:9] + v[9:10]) for v in blocks] + [square, jnp.zeros((8, 128), F32)]
    r4[row] = jnp.concatenate(rows, axis=0).astype(BF16)
    for to in row_peers:
        send(r4.at[row], r4.at[row], ssem.at[4], rowsem.at[row], (head, to))
    arrived(r3.at[0:3], ssem.at[3])

    which_row = lax.div(iota((1, 128), 1), 32)
    arrived(wo.at[1 - core], crecv)

    def onward(peers):
        rows = []
        for peer in peers:
            block = r4[peer].astype(F32)
            rows.append(jnp.concatenate([block[n * 8 : n * 8 + 8] for n in range(4)], axis=1))
            for p in range(2):
                square = block[32 + p * 4 : 33 + p * 4]
                for n in range(1, 4):
                    square = jnp.where(which_row == n, block[32 + p * 4 + n : 33 + p * 4 + n], square)
                sq[2 * peer + p] = square
        left_side = jnp.concatenate(rows, axis=0).astype(BF16)
        outs = [dot(left_side, wo[n]) for n in range(2)]
        for b, peer in enumerate(peers):
            for p in range(2):
                to = 2 * peer + p
                for k in range(4):
                    at = b * 8 + p * 4
                    f5[to, pl.ds(k, 4, stride=4), :] = outs[k // 2][at : at + 4, k % 2 * 128 : k % 2 * 128 + 128]
                s5[to] = f5[to].astype(BF16)

                @pl.when(to != quad)
                def _():
                    send(sq.at[to], rq.at[quad], qsend, qrecv, (to * 4 + place, row))
                    send(s5.at[to], r5.at[quad], xsend, xrecv, (to * 4 + place, row))

    onward([row])
    for peers in (row_peers[5:7], row_peers[3:5], row_peers[1:3], row_peers[0:1]):
        for peer in peers:
            arrived(r4.at[peer], rowsem.at[peer])
        onward(peers)
    for r in range(8, 16):
        update(r)
    rq[quad] = sq[quad]
    r5[quad] = s5[quad]
    arrived(r4.at[0:7], ssem.at[4])
    arrived(wo.at[core], csend)

    @pl.when(grp == bc_group)
    def _():
        arrived(rc.at[0:7], ssem.at[2])

    @pl.when(grp != bc_group)
    def _():
        arrived(rc, ssem.at[2])

    arrived(r5.at[0:15], xsend)
    arrived(r5.at[0:15], xrecv)
    arrived(rq.at[0:15], qsend)
    arrived(rq.at[0:15], qrecv)
    parts[...] = r5[...]
    squares[...] = rq[...]


def hand_over(parts, squares, a, b, c, layer_out, oa, ob, oc, made, o5, sem):
    moves = [(a.at[4 * n : 4 * n + 4], oa.at[4 * n : 4 * n + 4]) for n in range(4)] + [(b, ob), (c, oc)]
    copies = [pltpu.make_async_copy(src, dst, sem.at[n]) for n, (src, dst) in enumerate(moves)]
    for copy in copies:
        copy.start()
    total = jnp.zeros((16, 128), F32)
    mine = lax.div(iota((16, 128), 0), 4) * 32 == iota((16, 128), 1)
    for i in range(8):
        both = parts[2 * i].astype(F32) + parts[2 * i + 1].astype(F32)
        scale = lax.rsqrt((squares[2 * i] + squares[2 * i + 1]) / 1024.0 + EPS)
        total += both * jnp.sum(jnp.where(mine, scale, 0.0), axis=1, keepdims=True)
    o5[...] = total
    for s in range(2):
        for k in range(4):
            pair = o5[pl.ds(s * 8 + k, 2, stride=4), :]
            made[s, :, k * 128 : k * 128 + 128] = pair.astype(BF16)
    last = pltpu.make_async_copy(made, layer_out, sem.at[6])
    last.start()
    for copy in copies:
        copy.wait()
    last.wait()


def local(
    tokens, w_zx, w_bc, w_dt, conv_wx, conv_bx, conv_wbc, conv_bbc,
    dt_bias, decay_rate, skip_gain, norm_gain, w_out, ssm_state, tail_x, tail_bc,
):
    hbm = pl.BlockSpec(memory_space=pltpu.HBM)
    vmem = pl.BlockSpec(memory_space=pltpu.VMEM)
    V = pltpu.VMEM
    dma = pltpu.SemaphoreType.DMA
    shapes = (
        jax.ShapeDtypeStruct((2, 2, 512), BF16),
        jax.ShapeDtypeStruct((16, 128, 128), F32),
        jax.ShapeDtypeStruct((3, 16, 128), BF16),
        jax.ShapeDtypeStruct((3, 16, 32), BF16),
    )
    operands = (
        tokens,
        w_zx.reshape(1024, 128),
        w_bc.T,
        w_dt.T,
        w_out,
        ssm_state.reshape(16, 128, 128),
        conv_wx,
        conv_bx.reshape(1, 128),
        conv_wbc,
        conv_bbc.reshape(1, 32),
        dt_bias.reshape(1, 2),
        decay_rate.reshape(1, 2),
        skip_gain.reshape(1, 2),
        norm_gain.reshape(1, 128),
        jnp.transpose(tail_x, (1, 0, 2)),
        jnp.transpose(tail_bc, (1, 0, 2)),
    )
    made = pl.pallas_call(
        kernel,
        out_shape=(V((16, 16, 128), BF16), V((16, 1, 128), F32), *(V(v.shape, v.dtype) for v in shapes[1:])),
        in_specs=[hbm] * 16,
        out_specs=(vmem,) * 5,
        scratch_shapes=[
            V((2, 128, 512), BF16),
            V((1024, 128), BF16),
            V((32, 512), BF16),
            V((2, 512), BF16),
            V((16, 128, 128), F32),
            V((4, 128), F32),
            V((1, 128), F32),
            V((4, 32), F32),
            V((1, 32), F32),
            V((1, 2), F32),
            V((1, 2), F32),
            V((1, 2), F32),
            V((1, 128), F32),
            V((3, 16, 128), BF16),
            V((3, 16, 32), BF16),
            V((1024, 128), F32),
            V((128, 512), BF16),
            V((512, 256), BF16),
            V((8, 16, 128), BF16),
            V((8, 16, 128), BF16),
            V((8, 2, 32, 128), BF16),
            V((8, 2, 32, 128), BF16),
            V((16, 128), BF16),
            V((8, 16, 128), BF16),
            V((4, 16, 128), F32),
            V((4, 16, 128), BF16),
            V((4, 16, 128), BF16),
            V((8, 48, 128), BF16),
            V((16, 16, 128), BF16),
            V((16, 16, 128), BF16),
            V((16, 1, 128), F32),
            V((16, 1, 128), F32),
            V((2, 512, 256), BF16),
            V((32, 128), F32),
            V((16, 16, 128), F32),
            V((128, 2048), BF16),
            dma((15,)),
            dma((5,)),
            dma((5,)),
            dma,
            dma,
            dma,
            dma,
            pltpu.SemaphoreType.REGULAR,
            pltpu.SemaphoreType.REGULAR,
            dma,
            dma,
            dma,
            dma,
            dma((8,)),
        ],
        compiler_params=pltpu.CompilerParams(
            collective_id=0, has_side_effects=True, vmem_limit_bytes=32 << 20
        ),
    )(*(pltpu.with_memory_space_constraint(v, pltpu.HBM) for v in operands))
    outs = pl.pallas_call(
        hand_over,
        out_shape=shapes,
        in_specs=[vmem, vmem] + [pl.BlockSpec(memory_space=pl.ANY)] * 3,
        out_specs=(hbm,) * 4,
        scratch_shapes=[V((2, 2, 512), BF16), V((16, 128), F32), dma((7,))],
        compiler_params=pltpu.CompilerParams(vmem_limit_bytes=32 << 20),
    )(*made)
    back = (1, 0, 2)
    return outs[0], outs[1].reshape(16, 2, 64, 128), jnp.transpose(outs[2], back), jnp.transpose(outs[3], back)


def solution(mesh):
    placed = (
        P(None, None, "row"),
        P("row", None, "head"),
        P("row", "head"),
        P("row", "head"),
        P(None, "head"),
        P("head"),
        P(None, "head"),
        P("head"),
        P("head"),
        P("head"),
        P("head"),
        P("head"),
        P("head", "row"),
        P("row", "head", None, None),
        P("row", None, "head"),
        P("row", None, "head"),
    )
    return jax.shard_map(
        local,
        mesh=mesh,
        in_specs=placed,
        out_specs=(
            P(None, "head", "row"),
            P("row", "head", None, None),
            P("row", None, "head"),
            P("row", None, "head"),
        ),
        check_vma=False,
    )
```
